128 devices in a mesh: tensor: 16 (over z_lo, y, core), dp: 8 (over z_hi, x).
Axes of the slice: x: 4, y: 4, z: 4 (z_hi: 2, z_lo: 2; z = z_hi * 2 + z_lo), core: 2. Of those that a mesh axis runs over, the one named last changes fastest.
Arguments:
- inputs: bfloat16 [8, 640, 4096], P('dp', 'tensor'), may hold values from -6 to 6
- out_grad: bfloat16 [8, 640, 4096], P('dp', 'tensor'), may hold values from -6 to 6
- w_gate: bfloat16 [4096, 14336], P(None, 'tensor'), may hold values from -0.09375 to 0.09375
- w_up: bfloat16 [4096, 14336], P(None, 'tensor'), may hold values from -0.09375 to 0.09375
- w_down: bfloat16 [14336, 4096], P('tensor'), may hold values from -0.046875 to 0.046875
Outputs:
- input_grad: bfloat16 [8, 640, 4096], P('dp', 'tensor')
- grad_gate: bfloat16 [4096, 14336], P('dp', 'tensor')
- grad_up: bfloat16 [4096, 14336], P('dp', 'tensor')
- grad_down: bfloat16 [14336, 4096], P('tensor', 'dp')
The draws below stay inside these ranges and needn't reach their ends.
All inputs are finite; a program needn't handle non-finite values.
Results may differ from the reference program's by a relative error of at most 0.023.
Values may be sent and summed in bfloat16 or wider, within the bound.
A program may use at most 192 MiB of HBM per device.

```python
import math
import jax
import jax.numpy as jnp
from jax import lax

D = 4096
FF = 14336
SLAB = 640
N_DP = 8


def level_of(stream_key, shape, shards, smallest, high):
    def one(dim, parts):
        draws = jax.random.uniform(jax.random.fold_in(jax.random.fold_in(stream_key, 6), dim), (parts,), jnp.float32, smallest / len(shards), high / len(shards))
        return jnp.repeat(jnp.exp(draws), shape[dim] // parts).reshape((-1,) + (1,) * (len(shape) - dim - 1))

    factor_of = one(*shards[0])
    for cut in shards[1:]:
        factor_of = factor_of * one(*cut)
    return factor_of


def gaussian(key, shape, scale, limit, cuts=(), held_as=jnp.bfloat16):
    gain = level_of(key, shape, cuts, -0.22, 0.18) if cuts else 1.0
    values = jax.random.normal(key, shape, jnp.float32) * scale * gain
    return jnp.minimum(jnp.maximum(values, -limit), limit).astype(held_as)


def setup_inputs(seed: int = 0) -> dict:
    key_of = jax.random.split(jax.random.key(seed), 6)
    return {
        "inputs": gaussian(key_of[0], (N_DP, SLAB, D), 1.0, 6.0, ((0, 8), (1, 16))),
        "out_grad": gaussian(key_of[1], (N_DP, SLAB, D), 1.0, 6.0, ((0, 8), (1, 16))),
        "w_gate": gaussian(key_of[2], (D, FF), D ** -0.5, 0.09375, ((1, 16),)),
        "w_up": gaussian(key_of[3], (D, FF), D ** -0.5, 0.09375, ((1, 16),)),
        "w_down": gaussian(key_of[4], (FF, D), FF ** -0.5, 0.046875, ((0, 16),)),
    }


def rounded(value):
    low = lax.optimization_barrier(value.astype(jnp.bfloat16))
    return low.astype(jnp.float32)

def reference(inputs, out_grad, w_gate, w_up, w_down):
    scale_factor = 1.0 / math.sqrt(SLAB * N_DP)
    total_gate = jnp.zeros((D, FF), jnp.float32)
    total_up = jnp.zeros((D, FF), jnp.float32)
    total_down = jnp.zeros((FF, D), jnp.float32)
    slab_results = []
    for group in range(N_DP):
        slab_in = inputs[group]
        slab_grad = out_grad[group]
        gate = jnp.dot(slab_in, w_gate, preferred_element_type=jnp.float32)
        up = jnp.dot(slab_in, w_up, preferred_element_type=jnp.float32)
        sigmoid_gate = jax.nn.sigmoid(gate)
        hidden = (gate * sigmoid_gate * up).astype(jnp.bfloat16)
        hidden_grad = jnp.dot(slab_grad, w_down.T, preferred_element_type=jnp.float32)
        gate_grad = (hidden_grad * up * sigmoid_gate * (1.0 + gate * (1.0 - sigmoid_gate))).astype(jnp.bfloat16)
        up_grad = (hidden_grad * gate * sigmoid_gate).astype(jnp.bfloat16)
        back = jnp.dot(gate_grad, w_gate.T, preferred_element_type=jnp.float32)
        back = back + jnp.dot(up_grad, w_up.T, preferred_element_type=jnp.float32)
        slab_results.append(back.astype(jnp.bfloat16))
        total_gate = total_gate + rounded(jnp.dot(slab_in.T, gate_grad, preferred_element_type=jnp.float32))
        total_up = total_up + rounded(jnp.dot(slab_in.T, up_grad, preferred_element_type=jnp.float32))
        total_down = total_down + rounded(jnp.dot(hidden.T, slab_grad, preferred_element_type=jnp.float32))
    input_grad = jnp.stack(slab_results, axis=0)
    grad_gate = (total_gate * scale_factor).astype(jnp.bfloat16)
    grad_up = (total_up * scale_factor).astype(jnp.bfloat16)
    grad_down = (total_down * scale_factor).astype(jnp.bfloat16)
    return (input_grad, grad_gate, grad_up, grad_down)
```

```python
import functools
import math

import jax
import jax.numpy as jnp
from jax import lax
from jax.experimental import pallas as pl
from jax.experimental.pallas import tpu as pltpu
from jax.sharding import PartitionSpec as P

BF16 = jnp.bfloat16
F32 = jnp.float32
NX = NY = NZ = 4
NT = (((1,), (1,)), ((), ()))
HIDDEN, GATE, UP = 0, 1, 2
JOBS = ((HIDDEN, True), (HIDDEN, False), (GATE, True), (UP, True), (GATE, False), (UP, False))


def nt(left, right):
    return lax.dot_general(left, right, NT, preferred_element_type=F32)


def kernel(
    scale, x_in, g_in, wg_hbm, wu_hbm, wd_hbm,
    out_g, out_u, out_d, ig_main, ig_tail, p_hbm, s_hbm, r_hbm,
    xg, wg, wu, wd, fa, fb, lt, gu, own, fwd, got, pst, tail, ptail, fin, fin2,
    w_sem, core_ss, core_rs, ag_ss, ag_rs, sh_ss, sh_rs, x_ss, x_rs,
    p_ss, p_rs, r_ss, r_rs, z_ss, z_rs, o_ss, o_rs, loc_sem, fetch_sem,
):
    rows, width = x_in.shape
    half = width // 2
    quarter = half // 2
    main = rows // 16 * 16
    rest = rows - main
    chip = 2 * rows
    tokens = xg.shape[1]
    plane = NZ * chip
    hid = lt.shape[1]
    pad = wg.shape[1]
    full = pad - 128
    block = width // 8

    t = lax.axis_index("tensor")
    d = lax.axis_index("dp")
    c = lax.rem(t, 2)
    y = lax.rem(t // 2, NY)
    zl = t // (2 * NY)
    x = lax.rem(d, NX)
    zh = d // NX
    z = 2 * zh + zl

    def dev(dx, yy, zz, cc):
        xx = lax.rem(x + dx + NX, NX)
        return {"tensor": (lax.rem(zz, 2) * NY + yy) * 2 + cc, "dp": (zz // 2) * NX + xx}

    def ring(v, off):
        return lax.rem(v + off + 4, 4)

    def frame(cc):
        return y + cc * (z - y), z + cc * (y - z)

    def slot(cc, uu, vv):
        yy, zz = uu + cc * (vv - uu), vv + cc * (uu - vv)
        return NZ * yy + zz

    def uv_dev(uu, vv):
        return dev(0, uu + c * (vv - uu), vv + c * (uu - vv), c)

    def at_rows(index, count=chip, offset=0):
        return pl.ds(pl.multiple_of(chip * index + offset, 16), count)

    partner = dev(0, y, z, 1 - c)
    right, left = dev(1, y, z, c), dev(-1, y, z, c)
    across = dev(0, y, ring(z, 2), c)
    pending = []

    def rcopy(src, dst, ss, rs, to):
        return pltpu.make_async_remote_copy(
            src_ref=src, dst_ref=dst, send_sem=ss, recv_sem=rs,
            device_id=to, device_id_type=pl.DeviceIdType.MESH,
        )

    def send(src, dst, ss, rs, to):
        copy = rcopy(src, dst, ss, rs, to)
        copy.start()
        pending.append(copy)
        return copy

    first = pl.ds(pl.multiple_of(zh * full, 128), full)
    shared = pl.ds(2 * full, pad - full)
    loads = [
        pltpu.make_async_copy(wg_hbm.at[:, first], wg.at[:, pl.ds(0, full)], w_sem.at[0]),
        pltpu.make_async_copy(wg_hbm.at[:, shared], wg.at[:, pl.ds(full, pad - full)], w_sem.at[1]),
        pltpu.make_async_copy(wu_hbm.at[:, first], wu.at[:, pl.ds(0, full)], w_sem.at[2]),
        pltpu.make_async_copy(wu_hbm.at[:, shared], wu.at[:, pl.ds(full, pad - full)], w_sem.at[3]),
        pltpu.make_async_copy(wd_hbm.at[first, :], wd.at[pl.ds(0, full), :], w_sem.at[4]),
        pltpu.make_async_copy(wd_hbm.at[shared, :], wd.at[pl.ds(full, pad - full), :], w_sem.at[5]),
    ]
    for load in loads:
        load.start()

    barrier = pltpu.get_barrier_semaphore()
    greeted = [partner, right, left]
    for ry in range(NY):
        for rz in range(NZ):
            if ry or rz:
                greeted.append(dev(0, ring(y, ry), ring(z, rz), c))
    for to in greeted:
        pl.semaphore_signal(barrier, inc=1, device_id=to, device_id_type=pl.DeviceIdType.MESH)

    me = NZ * y + z
    for a, src in enumerate((x_in, g_in)):
        xg[a, at_rows(me, main, main * c), :] = src[0:main, :]
        last = src[main:rows, :].astype(F32)
        none = jnp.zeros_like(last)
        tail[a] = jnp.concatenate(
            [jnp.where(c == 0, last, none), jnp.where(c == 0, none, last)], axis=0
        ).astype(BF16)
    pl.semaphore_wait(barrier, len(greeted))

    for a in range(2):
        mine = xg.at[a, at_rows(me, main, main * c), :]
        send(mine, mine, core_ss.at[a, 0], core_rs.at[a, 0], partner)
        send(tail.at[a], ptail.at[a], core_ss.at[a, 1], core_rs.at[a, 1], partner)

    u, v = frame(c)
    pu, pv = frame(1 - c)
    GROUPS = (0, -1, 1, 2)

    def region(a, ou, ov, part=None):
        col = c * half if part is None else c * half + part * quarter
        return xg.at[
            a, at_rows(slot(c, ring(u, ou), ring(v, ov))),
            pl.ds(pl.multiple_of(col, quarter), half if part is None else quarter),
        ]

    def partner_region(a, ou, ov):
        return xg.at[
            a, at_rows(slot(1 - c, ring(pu, ou), ring(pv, ov))),
            pl.ds(pl.multiple_of((1 - c) * half, quarter), half),
        ]

    def place(label):
        if label < 4:
            base, kind, axis = 0, label, 0
        else:
            base, kind, axis = GROUPS[(label - 4) // 4], label % 4, 1
        off = (-1, 1, 2, 2)[kind]
        part = (None, None, 0, 1)[kind]
        return (off, 0, part) if axis == 0 else (base, off, part)

    def arrived(a, label):
        where = region(a, *place(label))
        rcopy(where, where, ag_ss.at[a, label], ag_rs.at[a, label], partner).wait_recv()

    def pass_on(a, label, where, to):
        send(where, where, ag_ss.at[a, label], ag_rs.at[a, label], to)

    u_plus, u_minus = uv_dev(ring(u, 1), v), uv_dev(ring(u, -1), v)
    v_plus, v_minus = uv_dev(u, ring(v, 1)), uv_dev(u, ring(v, -1))

    def share(a, ou, ov):
        n = 4 * (ou % 4) + ov % 4
        where = region(a, ou, ov)
        send(where, where, sh_ss.at[a, n], sh_rs.at[a, n], partner)

    def along_v(a, r):
        where = region(a, GROUPS[r], 0)
        pass_on(a, 4 + 4 * r, where, v_plus)
        pass_on(a, 5 + 4 * r, where, v_minus)

    def gather_steps(a):
        def begin():
            mine = xg.at[a, at_rows(me, main, main * (1 - c)), :]
            rcopy(mine, mine, core_ss.at[a, 0], core_rs.at[a, 0], partner).wait_recv()
            rcopy(tail.at[a], ptail.at[a], core_ss.at[a, 1], core_rs.at[a, 1], partner).wait_recv()
            xg[a, at_rows(me, 2 * rest, 2 * main), :] = tail[a] + ptail[a]
            where = region(a, 0, 0)
            pass_on(a, 0, where, u_plus)
            pass_on(a, 1, where, u_minus)
            along_v(a, 0)

        def u_step(kind):
            off = (-1, 1)[kind]
            arrived(a, kind)
            pass_on(a, 2 + kind, region(a, off, 0, kind), (u_plus, u_minus)[kind])
            along_v(a, 1 + kind)
            share(a, off, 0)

        def u_last():
            arrived(a, 2)
            arrived(a, 3)
            along_v(a, 3)
            share(a, 2, 0)

        def v_step(r, kind):
            off = (-1, 1)[kind]
            arrived(a, 4 + 4 * r + kind)
            pass_on(a, 6 + 4 * r + kind, region(a, GROUPS[r], off, kind), (v_plus, v_minus)[kind])
            share(a, GROUPS[r], off)

        def v_last(r):
            arrived(a, 6 + 4 * r)
            arrived(a, 7 + 4 * r)
            share(a, GROUPS[r], 2)

        def take():
            for ou in range(4):
                for ov in range(4):
                    if ou or ov:
                        n = 4 * ou + ov
                        where = partner_region(a, ou, ov)
                        rcopy(where, where, sh_ss.at[a, n], sh_rs.at[a, n], partner).wait_recv()

        steps = [begin, functools.partial(u_step, 0), functools.partial(u_step, 1), u_last]
        for r in range(4):
            steps += [functools.partial(v_step, r, 0), functools.partial(v_step, r, 1)]
            if r:
                steps.append(functools.partial(v_last, r - 1))
        steps += [functools.partial(v_last, 3), take]
        return steps

    steps_x, steps_g = gather_steps(0), gather_steps(1)
    steps_x[0]()
    steps_g[0]()
    for step in steps_x[1:4]:
        step()
    for step in steps_g[1:4]:
        step()
    for step in steps_x[4:]:
        step()
    later = steps_g[4:]

    for load in loads[:4]:
        load.wait()
    piece = 256

    def put_transposed(which, n, span, value):
        turned = value.T
        if n == 0:
            lt[which, 0:piece, span] = turned
        else:
            keep = full - piece
            lt[which, piece:full, span] = turned[0:keep]
            side = hid - full
            lt[which, full:hid, span] = jnp.where(
                zh == 0, turned[keep:keep + side], turned[keep + side:keep + 2 * side]
            )

    def gate_piece(i):
        span = pl.ds(pl.multiple_of(i * piece, piece), piece)
        slab = xg[0, span, :]
        for n in range(2):
            cols = pl.ds(n * piece, piece)
            gate = jnp.dot(slab, wg[:, cols], preferred_element_type=F32)
            up = jnp.dot(slab, wu[:, cols], preferred_element_type=F32)
            sig = jax.nn.sigmoid(gate)
            act = gate * sig
            fb[span, cols] = act.astype(BF16)
            fa[span, cols] = (up * sig * (1.0 + gate * (1.0 - sig))).astype(BF16)
            put_transposed(HIDDEN, n, span, (act * up).astype(BF16))

    pieces = tokens // piece
    done = 0
    for i in range(pieces):
        gate_piece(i)
        until = len(later) * (i + 1) // pieces
        for step in later[done:until]:
            step()
        done = until

    def factors(j, xx):
        which, other = JOBS[j]
        side = 1 - zh if other else zh
        col = pl.multiple_of(side * half + lax.rem(xx, NX) * block, block)
        return jnp.dot(
            lt[which], xg[1 if which == HIDDEN else 0, :, pl.ds(col, block)],
            preferred_element_type=F32,
        )

    top, low = pl.ds(0, hid // 2), pl.ds(hid // 2, hid // 2)
    R, OPP, L = 0, 1, 2
    opposite = {}

    def multiply(j):
        def one(s, carry):
            own[j, s] = factors(j, x + 1 + s).astype(BF16)
            return carry

        lax.fori_loop(0, 3, one, 0)
        opposite[j] = [
            rcopy(own.at[j, OPP, top], fwd.at[j, 0], x_ss.at[j, 0], x_rs.at[j, 0], right),
            rcopy(own.at[j, OPP, low], fwd.at[j, 1], x_ss.at[j, 1], x_rs.at[j, 1], left),
        ]
        for copy in opposite[j]:
            copy.start()
        send(own.at[j, R, low], got.at[j, 0, low], x_ss.at[j, 2], x_rs.at[j, 2], right)
        send(own.at[j, L, top], got.at[j, 1, top], x_ss.at[j, 3], x_rs.at[j, 3], left)

    def add_on(j):
        for n, (s, part, to) in enumerate(((R, top, right), (L, low, left))):
            rcopy(fwd.at[j, n], fwd.at[j, n], x_ss.at[j, n], x_rs.at[j, n], partner).wait_recv()
            own[j, s, part] = (own[j, s, part].astype(F32) + fwd[j, n].astype(F32)).astype(BF16)
            send(own.at[j, s, part], got.at[j, n, part], x_ss.at[j, 4 + n], x_rs.at[j, 4 + n], to)

    out_rows = (
        (pl.ds(0, full), pl.ds(pl.multiple_of(zh * full, 64), full)),
        (pl.ds(full, hid - full), pl.ds(pl.multiple_of(2 * full + zh * (hid - full), 64), hid - full)),
    )
    in_rows = (
        pl.ds(pl.multiple_of((1 - zh) * full, 64), full),
        pl.ds(pl.multiple_of(2 * full + (1 - zh) * (hid - full), 64), hid - full),
    )
    outs = {HIDDEN: out_d, GATE: out_g, UP: out_u}
    local = []

    def finish(j):
        which, other = JOBS[j]
        total = factors(j, x)
        for n, (a, b) in enumerate(((top, low), (low, top))):
            rcopy(got.at[j, n, b], got.at[j, n, b], x_ss.at[j, 2 + n], x_rs.at[j, 2 + n], partner).wait_recv()
            rcopy(got.at[j, n, a], got.at[j, n, a], x_ss.at[j, 4 + n], x_rs.at[j, 4 + n], partner).wait_recv()
        for n in range(2):
            total += got[j, n].astype(F32)
        for copy in opposite[j]:
            copy.wait_send()
        own[j, OPP] = (total * scale).astype(BF16)
        for n, (here, there) in enumerate(out_rows):
            if other:
                send(own.at[j, OPP, here], outs[which].at[there, :], z_ss.at[which, n], z_rs.at[which, n], across)
            else:
                copy = pltpu.make_async_copy(own.at[j, OPP, here], outs[which].at[there, :], loc_sem.at[which, n])
                copy.start()
                local.append(copy)

    multiply(0)
    multiply(1)

    loads[4].wait()
    loads[5].wait()

    def grad_piece(i, carry):
        span = pl.ds(pl.multiple_of(i * piece, piece), piece)
        slab = xg[1, span, :]
        for n in range(2):
            cols = pl.ds(n * piece, piece)
            back = nt(slab, wd[cols, :])
            gate_grad = (back * fa[span, cols].astype(F32)).astype(BF16)
            up_grad = (back * fb[span, cols].astype(F32)).astype(BF16)
            put_transposed(GATE, n, span, gate_grad)
            put_transposed(UP, n, span, up_grad)
            if n:
                lane = lax.broadcasted_iota(jnp.int32, (piece, piece), 1) - (full - piece)
                side = hid - full
                valid = (lane < 0) | ((lane >= side * zh) & (lane < side * (zh + 1)))
                gate_grad = jnp.where(valid, gate_grad, jnp.zeros_like(gate_grad))
                up_grad = jnp.where(valid, up_grad, jnp.zeros_like(up_grad))
            gu[0, span, cols] = gate_grad
            gu[1, span, cols] = up_grad
        return carry

    lax.fori_loop(0, pieces, grad_piece, 0)

    add_on(0)
    multiply(2)
    add_on(1)
    multiply(3)

    order = (2, 1, 3, 0)
    strip = 512

    def plane_rows(r):
        return pl.ds(pl.multiple_of(plane * ring(y, r), 16), plane)

    def staged(k):
        return wd.at[pl.ds(0, plane), pl.ds((k % 2) * half, half)]

    def back_piece(r, k, side, add):
        def one(n, carry):
            at = pl.ds(pl.multiple_of(side * half + n * strip, strip), strip)
            value = nt(gu[0, plane_rows(r), :], wg[at, :]) + nt(gu[1, plane_rows(r), :], wu[at, :])
            if add:
                value += pst[:, pl.ds(pl.multiple_of(n * strip, strip), strip)].astype(F32)
            wd[pl.ds(0, plane), pl.ds(pl.multiple_of((k % 2) * half + n * strip, strip), strip)] = value.astype(BF16)
            return carry

        lax.fori_loop(0, half // strip, one, 0)

    to_partner = []
    for k, r in enumerate(order):
        if k >= 2:
            to_partner[k - 2].wait_send()
        back_piece(r, k, 1 - c, False)
        copy = rcopy(staged(k), p_hbm.at[plane_rows(r), :], p_ss.at[k], p_rs.at[k], partner)
        copy.start()
        to_partner.append(copy)
    add_on(2)
    multiply(4)
    multiply(5)
    to_partner[2].wait_send()
    to_partner[3].wait_send()
    add_on(3)

    def spread(r):
        for rz in (2, 1, 3, 0):
            if r or rz:
                q = 4 * r + rz
                to = dev(0, ring(y, r), ring(z, rz), c)
                index = NZ * ring(y, r) + ring(z, rz)
                send(s_hbm.at[at_rows(index), :], r_hbm.at[q], r_ss.at[q], r_rs.at[q], to)

    written = []
    for k, r in enumerate(order):
        rcopy(staged(k), p_hbm.at[plane_rows(r), :], p_ss.at[k], p_rs.at[k], partner).wait_recv()
        fetch = pltpu.make_async_copy(p_hbm.at[plane_rows(r), :], pst, fetch_sem.at[0])
        fetch.start()
        fetch.wait()
        back_piece(r, k, c, True)
        copy = pltpu.make_async_copy(staged(k), s_hbm.at[plane_rows(r), :], fetch_sem.at[1])
        copy.start()
        copy.wait()
        spread(r)

    finish(0)
    add_on(4)
    finish(1)
    add_on(5)
    finish(2)
    finish(3)

    def held(k):
        return wd.at[pl.ds(chip * (k // 2), chip), pl.ds((k % 2) * half, half)]

    total = None
    for part in range(2):
        fetches = []
        for k in range(8):
            q = 8 * part + k
            if q:
                rcopy(r_hbm.at[q], r_hbm.at[q], r_ss.at[q], r_rs.at[q], partner).wait_recv()
                src = r_hbm.at[q]
            else:
                src = s_hbm.at[at_rows(me), :]
            fetches.append(pltpu.make_async_copy(src, held(k), fetch_sem.at[2 + k]))
            fetches[-1].start()
        for fetch in fetches:
            fetch.wait()
        for n in range(4):
            span = half // 4
            sum_ = None
            for k in range(8):
                at = pl.ds((k % 2) * half + n * span, span)
                term = wd[pl.ds(chip * (k // 2), chip), at].astype(F32)
                sum_ = term if sum_ is None else sum_ + term
            at = pl.ds(n * span, span)
            if part == 0:
                fin[0:chip, at] = sum_
            else:
                fin2[0:chip, at] = (fin[0:chip, at] + sum_).astype(BF16)

    mine = pl.ds(pl.multiple_of(c * half, half), half)
    theirs = pl.ds(pl.multiple_of((1 - c) * half, half), half)
    keep = fin2.at[pl.ds(pl.multiple_of(main * c, 16), main), :]
    give = fin2.at[pl.ds(pl.multiple_of(main * (1 - c), 16), main), :]
    ends = fin2.at[pl.ds(2 * main, 2 * rest), :]
    send(give, ig_main.at[:, mine], o_ss.at[0], o_rs.at[0], partner)
    send(ends, ig_tail.at[:, mine], o_ss.at[1], o_rs.at[1], partner)
    for n, (src, dst) in enumerate(((keep, ig_main.at[:, mine]), (ends, ig_tail.at[:, mine]))):
        copy = pltpu.make_async_copy(src, dst, fetch_sem.at[n])
        copy.start()
        local.append(copy)

    finish(4)
    finish(5)

    for n, (src, dst) in enumerate(((keep, ig_main), (ends, ig_tail))):
        rcopy(src, dst.at[:, theirs], o_ss.at[n], o_rs.at[n], partner).wait_recv()
    for which in (HIDDEN, GATE, UP):
        for n, (here, _) in enumerate(out_rows):
            rcopy(own.at[0, OPP, here], outs[which].at[in_rows[n], :], z_ss.at[which, n], z_rs.at[which, n], partner).wait_recv()
    for copy in pending:
        copy.wait_send()
    for copy in local:
        copy.wait()


def local(inputs, out_grad, w_gate, w_up, w_down):
    _, rows, width = inputs.shape
    units = w_gate.shape[1]
    hid = units // 2
    pad = hid + 64
    tokens = 2 * rows * NY * NZ
    half = width // 2
    block = width // 8
    chip = 2 * rows
    scale = 1.0 / math.sqrt(rows * lax.axis_size("tensor") * lax.axis_size("dp"))
    dma = pltpu.SemaphoreType.DMA
    any_ = pl.BlockSpec(memory_space=pl.ANY)
    vmem = pl.BlockSpec(memory_space=pltpu.VMEM)
    arr = lambda *shape: jax.ShapeDtypeStruct(shape, BF16)
    outs = pl.pallas_call(
        functools.partial(kernel, scale),
        out_shape=(
            arr(units, block), arr(units, block), arr(units, block),
            arr(rows // 16 * 16, width), arr(16, width),
            arr(tokens, half), arr(tokens, half), arr(NY * NZ, chip, half),
        ),
        in_specs=[vmem, vmem, any_, any_, any_],
        out_specs=(any_,) * 8,
        scratch_shapes=[
            pltpu.VMEM((2, tokens, width), BF16),
            pltpu.VMEM((width, pad), BF16),
            pltpu.VMEM((width, pad), BF16),
            pltpu.VMEM((pad, width), BF16),
            pltpu.VMEM((tokens, pad), BF16),
            pltpu.VMEM((tokens, pad), BF16),
            pltpu.VMEM((3, hid, tokens), BF16),
            pltpu.VMEM((2, tokens, pad), BF16),
            pltpu.VMEM((6, 3, hid, block), BF16),
            pltpu.VMEM((6, 2, hid // 2, block), BF16),
            pltpu.VMEM((6, 2, hid, block), BF16),
            pltpu.VMEM((NZ * chip, half), BF16),
            pltpu.VMEM((2, 16, width), BF16),
            pltpu.VMEM((2, 16, width), BF16),
            pltpu.VMEM((chip, half), F32),
            pltpu.VMEM((chip, half), BF16),
            dma((6,)), dma((2, 2)), dma((2, 2)),
            dma((2, 20)), dma((2, 20)), dma((2, 16)), dma((2, 16)),
            dma((6, 6)), dma((6, 6)),
            dma((4,)), dma((4,)), dma((16,)), dma((16,)),
            dma((3, 2)), dma((3, 2)), dma((2,)), dma((2,)),
            dma((3, 2)), dma((10,)),
        ],
        compiler_params=pltpu.CompilerParams(
            collective_id=0, has_side_effects=True, vmem_limit_bytes=63 * 2**20
        ),
        cost_estimate=pl.CostEstimate(
            flops=16 * tokens * width * hid, bytes_accessed=6 * width * units, transcendentals=tokens * hid
        ),
    )(inputs[0], out_grad[0], w_gate, w_up, w_down)
    grad_gate, grad_up, grad_down, ig_main, ig_tail = outs[:5]
    core = lax.rem(lax.axis_index("tensor"), 2)
    rest = rows - rows // 16 * 16
    ends = lax.dynamic_slice_in_dim(ig_tail, core * rest, rest, 0)
    input_grad = jnp.concatenate([ig_main, ends], axis=0)[None]
    return (input_grad, grad_gate.T, grad_up.T, grad_down)


def solution(mesh):
    placed = (
        P("dp", "tensor", None),
        P("dp", "tensor", None),
        P(None, "tensor"),
        P(None, "tensor"),
        P("tensor", None),
    )
    return jax.shard_map(
        local,
        mesh=mesh,
        in_specs=placed,
        out_specs=(
            P("dp", "tensor", None),
            P("dp", "tensor"),
            P("dp", "tensor"),
            P("tensor", "dp"),
        ),
        check_vma=False,
    )
```

```python
import functools
import math

import jax
import jax.numpy as jnp
from jax import lax
from jax.experimental import pallas as pl
from jax.experimental.pallas import tpu as pltpu
from jax.sharding import PartitionSpec as P

BF16 = jnp.bfloat16
F32 = jnp.float32
NX = NY = NZ = 4
NT = (((1,), (1,)), ((), ()))
HIDDEN, GATE, UP = 0, 1, 2
JOBS = ((HIDDEN, True), (GATE, True), (UP, True), (HIDDEN, False), (GATE, False), (UP, False))


def nt(left, right):
    return lax.dot_general(left, right, NT, preferred_element_type=F32)


def kernel(
    scale, x_in, g_in, wg_hbm, wu_hbm, wd_hbm,
    out_g, out_u, out_d, ig_main, ig_tail, p_hbm, s_hbm, r_hbm,
    xg, wg, wu, wd, fa, fb, lt, gu, own, fwd, got, sums, tail, ptail,
    w_sem, core_ss, core_rs, ag_ss, ag_rs, sh_ss, sh_rs, x_ss, x_rs,
    p_ss, p_rs, r_ss, r_rs, z_ss, z_rs, o_ss, o_rs, loc_sem, fetch_sem,
):
    rows, width = x_in.shape
    half = width // 2
    quarter = half // 2
    main = rows // 16 * 16
    rest = rows - main
    chip = 2 * rows
    tokens = xg.shape[1]
    plane = NZ * chip
    hid = lt.shape[1]
    pad = wg.shape[1]
    full = pad - 128
    block = width // 8

    t = lax.axis_index("tensor")
    d = lax.axis_index("dp")
    c = lax.rem(t, 2)
    y = lax.rem(t // 2, NY)
    zl = t // (2 * NY)
    x = lax.rem(d, NX)
    zh = d // NX
    z = 2 * zh + zl

    def dev(dx, yy, zz, cc):
        xx = lax.rem(x + dx + NX, NX)
        return {"tensor": (lax.rem(zz, 2) * NY + yy) * 2 + cc, "dp": (zz // 2) * NX + xx}

    def ring(v, off):
        return lax.rem(v + off + 4, 4)

    def frame(cc):
        return y + cc * (z - y), z + cc * (y - z)

    def slot(cc, uu, vv):
        yy, zz = uu + cc * (vv - uu), vv + cc * (uu - vv)
        return NZ * yy + zz

    def uv_dev(uu, vv):
        return dev(0, uu + c * (vv - uu), vv + c * (uu - vv), c)

    def at_rows(index, count=chip, offset=0):
        return pl.ds(pl.multiple_of(chip * index + offset, 16), count)

    partner = dev(0, y, z, 1 - c)
    right, left = dev(1, y, z, c), dev(-1, y, z, c)
    across = dev(0, y, ring(z, 2), c)
    pending = []

    def rcopy(src, dst, ss, rs, to):
        return pltpu.make_async_remote_copy(
            src_ref=src, dst_ref=dst, send_sem=ss, recv_sem=rs,
            device_id=to, device_id_type=pl.DeviceIdType.MESH,
        )

    def send(src, dst, ss, rs, to):
        copy = rcopy(src, dst, ss, rs, to)
        copy.start()
        pending.append(copy)
        return copy

    first = pl.ds(pl.multiple_of(zh * full, 128), full)
    shared = pl.ds(2 * full, pad - full)
    loads = [
        pltpu.make_async_copy(wg_hbm.at[:, first], wg.at[:, pl.ds(0, full)], w_sem.at[0]),
        pltpu.make_async_copy(wg_hbm.at[:, shared], wg.at[:, pl.ds(full, pad - full)], w_sem.at[1]),
        pltpu.make_async_copy(wu_hbm.at[:, first], wu.at[:, pl.ds(0, full)], w_sem.at[2]),
        pltpu.make_async_copy(wu_hbm.at[:, shared], wu.at[:, pl.ds(full, pad - full)], w_sem.at[3]),
        pltpu.make_async_copy(wd_hbm.at[first, :], wd.at[pl.ds(0, full), :], w_sem.at[4]),
        pltpu.make_async_copy(wd_hbm.at[shared, :], wd.at[pl.ds(full, pad - full), :], w_sem.at[5]),
    ]
    for load in loads:
        load.start()

    barrier = pltpu.get_barrier_semaphore()
    greeted = [partner, right, left]
    for ry in range(NY):
        for rz in range(NZ):
            if ry or rz:
                greeted.append(dev(0, ring(y, ry), ring(z, rz), c))
    for to in greeted:
        pl.semaphore_signal(barrier, inc=1, device_id=to, device_id_type=pl.DeviceIdType.MESH)

    me = NZ * y + z
    for a, src in enumerate((x_in, g_in)):
        xg[a, at_rows(me, main, main * c), :] = src[0:main, :]
        last = src[main:rows, :].astype(F32)
        none = jnp.zeros_like(last)
        tail[a] = jnp.concatenate(
            [jnp.where(c == 0, last, none), jnp.where(c == 0, none, last)], axis=0
        ).astype(BF16)
    pl.semaphore_wait(barrier, len(greeted))

    for a in range(2):
        mine = xg.at[a, at_rows(me, main, main * c), :]
        send(mine, mine, core_ss.at[a, 0], core_rs.at[a, 0], partner)
        send(tail.at[a], ptail.at[a], core_ss.at[a, 1], core_rs.at[a, 1], partner)

    u, v = frame(c)
    pu, pv = frame(1 - c)
    GROUPS = (0, -1, 1, 2)

    def region(a, ou, ov, part=None):
        col = c * half if part is None else c * half + part * quarter
        return xg.at[
            a, at_rows(slot(c, ring(u, ou), ring(v, ov))),
            pl.ds(pl.multiple_of(col, quarter), half if part is None else quarter),
        ]

    def partner_region(a, ou, ov):
        return xg.at[
            a, at_rows(slot(1 - c, ring(pu, ou), ring(pv, ov))),
            pl.ds(pl.multiple_of((1 - c) * half, quarter), half),
        ]

    def place(label):
        if label < 4:
            base, kind, axis = 0, label, 0
        else:
            base, kind, axis = GROUPS[(label - 4) // 4], label % 4, 1
        off = (-1, 1, 2, 2)[kind]
        part = (None, None, 0, 1)[kind]
        return (off, 0, part) if axis == 0 else (base, off, part)

    def arrived(a, label):
        where = region(a, *place(label))
        rcopy(where, where, ag_ss.at[a, label], ag_rs.at[a, label], partner).wait_recv()

    def pass_on(a, label, where, to):
        send(where, where, ag_ss.at[a, label], ag_rs.at[a, label], to)

    u_plus, u_minus = uv_dev(ring(u, 1), v), uv_dev(ring(u, -1), v)
    v_plus, v_minus = uv_dev(u, ring(v, 1)), uv_dev(u, ring(v, -1))

    def share(a, ou, ov):
        n = 4 * (ou % 4) + ov % 4
        where = region(a, ou, ov)
        send(where, where, sh_ss.at[a, n], sh_rs.at[a, n], partner)

    def along_v(a, r):
        where = region(a, GROUPS[r], 0)
        pass_on(a, 4 + 4 * r, where, v_plus)
        pass_on(a, 5 + 4 * r, where, v_minus)

    def gather_steps(a):
        def begin():
            mine = xg.at[a, at_rows(me, main, main * (1 - c)), :]
            rcopy(mine, mine, core_ss.at[a, 0], core_rs.at[a, 0], partner).wait_recv()
            rcopy(tail.at[a], ptail.at[a], core_ss.at[a, 1], core_rs.at[a, 1], partner).wait_recv()
            xg[a, at_rows(me, 2 * rest, 2 * main), :] = tail[a] + ptail[a]
            where = region(a, 0, 0)
            pass_on(a, 0, where, u_plus)
            pass_on(a, 1, where, u_minus)
            along_v(a, 0)

        def u_step(kind):
            off = (-1, 1)[kind]
            arrived(a, kind)
            pass_on(a, 2 + kind, region(a, off, 0, kind), (u_plus, u_minus)[kind])
            along_v(a, 1 + kind)
            share(a, off, 0)

        def u_last():
            arrived(a, 2)
            arrived(a, 3)
            along_v(a, 3)
            share(a, 2, 0)

        def v_step(r, kind):
            off = (-1, 1)[kind]
            arrived(a, 4 + 4 * r + kind)
            pass_on(a, 6 + 4 * r + kind, region(a, GROUPS[r], off, kind), (v_plus, v_minus)[kind])
            share(a, GROUPS[r], off)

        def v_last(r):
            arrived(a, 6 + 4 * r)
            arrived(a, 7 + 4 * r)
            share(a, GROUPS[r], 2)

        def take():
            for ou in range(4):
                for ov in range(4):
                    if ou or ov:
                        n = 4 * ou + ov
                        where = partner_region(a, ou, ov)
                        rcopy(where, where, sh_ss.at[a, n], sh_rs.at[a, n], partner).wait_recv()

        steps = [begin, functools.partial(u_step, 0), functools.partial(u_step, 1), u_last]
        for r in range(4):
            steps += [functools.partial(v_step, r, 0), functools.partial(v_step, r, 1)]
            if r:
                steps.append(functools.partial(v_last, r - 1))
        steps += [functools.partial(v_last, 3), take]
        return steps

    steps_x, steps_g = gather_steps(0), gather_steps(1)
    steps_x[0]()
    steps_g[0]()
    for step in steps_x[1:4]:
        step()
    for step in steps_g[1:4]:
        step()
    for step in steps_x[4:]:
        step()
    later = steps_g[4:]

    for load in loads[:4]:
        load.wait()
    piece = 256

    def put_transposed(which, n, span, value):
        turned = value.T
        if n == 0:
            lt[which, 0:piece, span] = turned
        else:
            keep = full - piece
            lt[which, piece:full, span] = turned[0:keep]
            side = hid - full
            lt[which, full:hid, span] = jnp.where(
                zh == 0, turned[keep:keep + side], turned[keep + side:keep + 2 * side]
            )

    def gate_piece(i):
        span = pl.ds(pl.multiple_of(i * piece, piece), piece)
        slab = xg[0, span, :]
        for n in range(2):
            cols = pl.ds(n * piece, piece)
            gate = jnp.dot(slab, wg[:, cols], preferred_element_type=F32)
            up = jnp.dot(slab, wu[:, cols], preferred_element_type=F32)
            sig = jax.nn.sigmoid(gate)
            act = gate * sig
            fb[span, cols] = act.astype(BF16)
            fa[span, cols] = (up * sig * (1.0 + gate * (1.0 - sig))).astype(BF16)
            put_transposed(HIDDEN, n, span, (act * up).astype(BF16))

    pieces = tokens // piece
    done = 0
    for i in range(pieces):
        gate_piece(i)
        until = len(later) * (i + 1) // pieces
        for step in later[done:until]:
            step()
        done = until

    def factors(j, xx):
        which, other = JOBS[j]
        side = 1 - zh if other else zh
        col = pl.multiple_of(side * half + lax.rem(xx, NX) * block, block)
        return jnp.dot(
            lt[which], xg[1 if which == HIDDEN else 0, :, pl.ds(col, block)],
            preferred_element_type=F32,
        )

    top, low = pl.ds(0, hid // 2), pl.ds(hid // 2, hid // 2)
    R, OPP, L = 0, 1, 2
    opposite = {}

    def multiply(j):
        def one(s, carry):
            own[j, s] = factors(j, x + 1 + s).astype(BF16)
            return carry

        lax.fori_loop(0, 3, one, 0)
        opposite[j] = [
            rcopy(own.at[j, OPP, top], fwd.at[j, 0], x_ss.at[j, 0], x_rs.at[j, 0], right),
            rcopy(own.at[j, OPP, low], fwd.at[j, 1], x_ss.at[j, 1], x_rs.at[j, 1], left),
        ]
        for copy in opposite[j]:
            copy.start()
        send(own.at[j, R, low], got.at[j, 0, low], x_ss.at[j, 2], x_rs.at[j, 2], right)
        send(own.at[j, L, top], got.at[j, 1, top], x_ss.at[j, 3], x_rs.at[j, 3], left)

    def add_on(j):
        for n, (s, part, to) in enumerate(((R, top, right), (L, low, left))):
            rcopy(fwd.at[j, n], fwd.at[j, n], x_ss.at[j, n], x_rs.at[j, n], partner).wait_recv()
            own[j, s, part] = (own[j, s, part].astype(F32) + fwd[j, n].astype(F32)).astype(BF16)
            send(own.at[j, s, part], got.at[j, n, part], x_ss.at[j, 4 + n], x_rs.at[j, 4 + n], to)

    out_rows = (
        (pl.ds(0, full), pl.ds(pl.multiple_of(zh * full, 64), full)),
        (pl.ds(full, hid - full), pl.ds(pl.multiple_of(2 * full + zh * (hid - full), 64), hid - full)),
    )
    in_rows = (
        pl.ds(pl.multiple_of((1 - zh) * full, 64), full),
        pl.ds(pl.multiple_of(2 * full + (1 - zh) * (hid - full), 64), hid - full),
    )
    outs = {HIDDEN: out_d, GATE: out_g, UP: out_u}
    local = []

    def finish(j):
        which, other = JOBS[j]
        total = factors(j, x)
        for n, (a, b) in enumerate(((top, low), (low, top))):
            rcopy(got.at[j, n, b], got.at[j, n, b], x_ss.at[j, 2 + n], x_rs.at[j, 2 + n], partner).wait_recv()
            rcopy(got.at[j, n, a], got.at[j, n, a], x_ss.at[j, 4 + n], x_rs.at[j, 4 + n], partner).wait_recv()
        for n in range(2):
            total += got[j, n].astype(F32)
        for copy in opposite[j]:
            copy.wait_send()
        own[j, OPP] = (total * scale).astype(BF16)
        for n, (here, there) in enumerate(out_rows):
            if other:
                send(own.at[j, OPP, here], outs[which].at[there, :], z_ss.at[which, n], z_rs.at[which, n], across)
            else:
                copy = pltpu.make_async_copy(own.at[j, OPP, here], outs[which].at[there, :], loc_sem.at[which, n])
                copy.start()
                local.append(copy)

    multiply(0)

    loads[4].wait()
    loads[5].wait()

    def grad_piece(i, carry):
        span = pl.ds(pl.multiple_of(i * piece, piece), piece)
        slab = xg[1, span, :]
        for n in range(2):
            cols = pl.ds(n * piece, piece)
            back = nt(slab, wd[cols, :])
            gate_grad = (back * fa[span, cols].astype(F32)).astype(BF16)
            up_grad = (back * fb[span, cols].astype(F32)).astype(BF16)
            put_transposed(GATE, n, span, gate_grad)
            put_transposed(UP, n, span, up_grad)
            if n:
                lane = lax.broadcasted_iota(jnp.int32, (piece, piece), 1) - (full - piece)
                side = hid - full
                valid = (lane < 0) | ((lane >= side * zh) & (lane < side * (zh + 1)))
                gate_grad = jnp.where(valid, gate_grad, jnp.zeros_like(gate_grad))
                up_grad = jnp.where(valid, up_grad, jnp.zeros_like(up_grad))
            gu[0, span, cols] = gate_grad
            gu[1, span, cols] = up_grad
        return carry

    lax.fori_loop(0, pieces, grad_piece, 0)

    multiply(1)
    add_on(0)
    multiply(2)

    order = (2, 1, 3, 0)
    strip = 512
    strips = half // strip

    def back_piece(k, cc, add):
        buf = (fa, fb)[k % 2]
        uu, vv = frame(cc)
        spans = [at_rows(slot(cc, ring(uu, order[k]), ring(vv, rv))) for rv in range(4)]

        def one(n, carry):
            at = pl.ds(pl.multiple_of(cc * half + n * strip, strip), strip)
            held = pl.ds(pl.multiple_of(n * plane, 16), plane)
            value = sum(
                nt(jnp.concatenate([gu[w, span, :] for span in spans], axis=0), weight[at, :])
                for w, weight in enumerate((wg, wu))
            )
            if add:
                value += buf[held, :].astype(F32)
                wd[0:plane, pl.ds(pl.multiple_of((k % 2) * half + n * strip, strip), strip)] = value.astype(BF16)
            else:
                buf[held, :] = value.astype(BF16)
            return carry

        lax.fori_loop(0, strips, one, 0)

    to_partner = []
    for k in range(4):
        if k >= 2:
            to_partner[k - 2].wait_send()
        back_piece(k, 1 - c, False)
        copy = rcopy((fa, fb)[k % 2], p_hbm.at[k], p_ss.at[k], p_rs.at[k], partner)
        copy.start()
        to_partner.append(copy)
    add_on(1)
    multiply(3)
    to_partner[2].wait_send()
    to_partner[3].wait_send()

    def fetch(k):
        rcopy(p_hbm.at[k], p_hbm.at[k], p_ss.at[k], p_rs.at[k], partner).wait_recv()
        copy = pltpu.make_async_copy(p_hbm.at[k], (fa, fb)[k % 2], fetch_sem.at[k % 2])
        copy.start()
        return copy

    def spread(k):
        for rv in (2, 1, 3):
            q = 3 * k + rv - 1
            src = s_hbm.at[k, pl.ds(chip * rv, chip), :]
            send(src, r_hbm.at[q], r_ss.at[q], r_rs.at[q], uv_dev(u, ring(v, rv)))

    fetched = [fetch(0), fetch(1)]
    written = []
    for k in range(4):
        fetched[k].wait()
        back_piece(k, c, True)
        copy = pltpu.make_async_copy(
            wd.at[pl.ds(0, plane), pl.ds((k % 2) * half, half)], s_hbm.at[k], fetch_sem.at[2 + k % 2]
        )
        copy.start()
        written.append(copy)
        if k + 2 < 4:
            fetched.append(fetch(k + 2))
        if k:
            written[k - 1].wait()
            spread(k - 1)
    written[3].wait()
    spread(3)

    add_on(2)
    multiply(4)
    add_on(3)
    multiply(5)
    finish(0)
    finish(1)

    def collect(arrivals, kept, k):
        places = [
            wd.at[pl.ds(chip * (n // 2 + 2 * (k % 2)), chip), pl.ds((n % 2) * half, half)] for n in range(4)
        ]
        copies = []
        for n, q in enumerate(arrivals):
            rcopy(r_hbm.at[q], r_hbm.at[q], r_ss.at[q], r_rs.at[q], partner).wait_recv()
            copies.append(pltpu.make_async_copy(r_hbm.at[q], places[n], fetch_sem.at[4 + n]))
        if kept is not None:
            copies.append(pltpu.make_async_copy(kept, places[3], fetch_sem.at[7]))
        for copy in copies:
            copy.start()
        for copy in copies:
            copy.wait()
        span = half // 4
        for n in range(4):
            at = pl.ds(n * span, span)
            terms = [place[:, at].astype(F32) for place in places[:len(copies)]]
            if kept is None:
                terms.append(sums[3, :, at].astype(F32))
            sums[k, :, at] = sum(terms).astype(BF16)

    for k in range(4):
        collect([3 * k, 3 * k + 1, 3 * k + 2], s_hbm.at[k, pl.ds(0, chip), :], k)
        r = order[k]
        if r:
            q = 11 + r
            send(sums.at[k], r_hbm.at[q], r_ss.at[q], r_rs.at[q], uv_dev(ring(u, r), v))
    add_on(4)
    finish(2)
    add_on(5)
    collect([12, 13, 14], None, 4)

    mine = pl.ds(pl.multiple_of(c * half, half), half)
    theirs = pl.ds(pl.multiple_of((1 - c) * half, half), half)
    keep = sums.at[4, pl.ds(pl.multiple_of(main * c, 16), main), :]
    give = sums.at[4, pl.ds(pl.multiple_of(main * (1 - c), 16), main), :]
    ends = sums.at[4, pl.ds(2 * main, 2 * rest), :]
    send(give, ig_main.at[:, mine], o_ss.at[0], o_rs.at[0], partner)
    send(ends, ig_tail.at[:, mine], o_ss.at[1], o_rs.at[1], partner)
    for n, (src, dst) in enumerate(((keep, ig_main.at[:, mine]), (ends, ig_tail.at[:, mine]))):
        copy = pltpu.make_async_copy(src, dst, fetch_sem.at[n])
        copy.start()
        local.append(copy)

    finish(3)
    finish(4)
    finish(5)

    for n, (src, dst) in enumerate(((keep, ig_main), (ends, ig_tail))):
        rcopy(src, dst.at[:, theirs], o_ss.at[n], o_rs.at[n], partner).wait_recv()
    for which in (HIDDEN, GATE, UP):
        for n, (here, _) in enumerate(out_rows):
            rcopy(own.at[0, OPP, here], outs[which].at[in_rows[n], :], z_ss.at[which, n], z_rs.at[which, n], partner).wait_recv()
    for copy in pending:
        copy.wait_send()
    for copy in local:
        copy.wait()


def arrange(gate_t, up_t, down, ig_main, ig_tail, grad_gate, grad_up, grad_down, input_grad, sem):
    move = pltpu.make_async_copy(down, grad_down, sem)
    move.start()
    main = ig_main.shape[0]
    rest = input_grad.shape[0] - main
    core = lax.rem(lax.axis_index("tensor"), 2)
    ends = ig_tail[...].astype(F32)
    input_grad[0:main, :] = ig_main[...]
    input_grad[main:, :] = jnp.where(core == 0, ends[0:rest], ends[rest:]).astype(BF16)
    for n in range(gate_t.shape[0] // 128):
        at = pl.ds(n * 128, 128)
        grad_gate[:, at] = gate_t[at, :].T
        grad_up[:, at] = up_t[at, :].T
    move.wait()


def local(inputs, out_grad, w_gate, w_up, w_down):
    _, rows, width = inputs.shape
    units = w_gate.shape[1]
    hid = units // 2
    pad = hid + 64
    tokens = 2 * rows * NY * NZ
    half = width // 2
    block = width // 8
    chip = 2 * rows
    scale = 1.0 / math.sqrt(rows * lax.axis_size("tensor") * lax.axis_size("dp"))
    dma = pltpu.SemaphoreType.DMA
    any_ = pl.BlockSpec(memory_space=pl.ANY)
    vmem = pl.BlockSpec(memory_space=pltpu.VMEM)
    arr = lambda *shape: jax.ShapeDtypeStruct(shape, BF16)
    outs = pl.pallas_call(
        functools.partial(kernel, scale),
        out_shape=(
            arr(units, block), arr(units, block), arr(units, block),
            arr(rows // 16 * 16, width), arr(16, width),
            arr(4, tokens, half // 4), arr(4, tokens // 4, half), arr(NY * NZ - 1, chip, half),
        ),
        in_specs=[vmem, vmem, any_, any_, any_],
        out_specs=(any_,) * 8,
        scratch_shapes=[
            pltpu.VMEM((2, tokens, width), BF16),
            pltpu.VMEM((width, pad), BF16),
            pltpu.VMEM((width, pad), BF16),
            pltpu.VMEM((pad, width), BF16),
            pltpu.VMEM((tokens, pad), BF16),
            pltpu.VMEM((tokens, pad), BF16),
            pltpu.VMEM((3, hid, tokens), BF16),
            pltpu.VMEM((2, tokens, pad), BF16),
            pltpu.VMEM((6, 3, hid, block), BF16),
            pltpu.VMEM((6, 2, hid // 2, block), BF16),
            pltpu.VMEM((6, 2, hid, block), BF16),
            pltpu.VMEM((5, chip, half), BF16),
            pltpu.VMEM((2, 16, width), BF16),
            pltpu.VMEM((2, 16, width), BF16),
            dma((6,)), dma((2, 2)), dma((2, 2)),
            dma((2, 20)), dma((2, 20)), dma((2, 16)), dma((2, 16)),
            dma((6, 6)), dma((6, 6)),
            dma((4,)), dma((4,)), dma((15,)), dma((15,)),
            dma((3, 2)), dma((3, 2)), dma((2,)), dma((2,)),
            dma((3, 2)), dma((8,)),
        ],
        compiler_params=pltpu.CompilerParams(
            collective_id=0, has_side_effects=True, vmem_limit_bytes=63 * 2**20
        ),
        cost_estimate=pl.CostEstimate(
            flops=16 * tokens * width * hid, bytes_accessed=6 * width * units, transcendentals=tokens * hid
        ),
    )(inputs[0], out_grad[0], w_gate, w_up, w_down)
    grad_gate, grad_up, grad_down, input_grad = pl.pallas_call(
        arrange,
        out_shape=(arr(block, units), arr(block, units), arr(units, block), arr(rows, width)),
        in_specs=[vmem, vmem, any_, vmem, vmem],
        out_specs=(vmem, vmem, any_, vmem),
        scratch_shapes=[dma(())],
    )(*outs[:5])
    return (input_grad[None], grad_gate, grad_up, grad_down)


def solution(mesh):
    placed = (
        P("dp", "tensor", None),
        P("dp", "tensor", None),
        P(None, "tensor"),
        P(None, "tensor"),
        P("tensor", None),
    )
    return jax.shard_map(
        local,
        mesh=mesh,
        in_specs=placed,
        out_specs=(
            P("dp", "tensor", None),
            P("dp", "tensor"),
            P("dp", "tensor"),
            P("tensor", "dp"),
        ),
        check_vma=False,
    )
```

```python
import functools
import math

import jax
import jax.numpy as jnp
from jax import lax
from jax.experimental import pallas as pl
from jax.experimental.pallas import tpu as pltpu
from jax.sharding import PartitionSpec as P

BF16 = jnp.bfloat16
F32 = jnp.float32
NX = NY = NZ = 4
NT = (((1,), (1,)), ((), ()))
HIDDEN, GATE, UP = 0, 1, 2
LOW, HIGH, OTHER, SAME = 0, 1, 2, 3
JOBS = ((HIDDEN, LOW), (HIDDEN, HIGH), (GATE, OTHER), (UP, OTHER), (GATE, SAME), (UP, SAME))
PARTS = ((0, 0, 2), (1, 0, 1), (1, 2, 1))


def nt(left, right):
    return lax.dot_general(left, right, NT, preferred_element_type=F32)


def kernel(
    scale, x_in, g_in, wg_hbm, wu_hbm, wd_hbm,
    out_g, out_u, out_d, ig_main, ig_tail, p_hbm, s_hbm, r_hbm,
    xg, wg, wu, wd, fa, fb, lt, gu, own, fwd, got, sums, pst, tail, ptail,
    w_sem, core_ss, core_rs, ag_ss, ag_rs, sh_ss, sh_rs, x_ss, x_rs,
    p_ss, p_rs, r_ss, r_rs, z_ss, z_rs, o_ss, o_rs, loc_sem, fetch_sem,
):
    rows, width = x_in.shape
    half = width // 2
    quarter = half // 2
    main = rows // 16 * 16
    rest = rows - main
    chip = 2 * rows
    tokens = xg.shape[1]
    plane = NZ * chip
    hid = lt.shape[1]
    pad = wg.shape[1]
    full = pad - 128
    block = width // 8

    t = lax.axis_index("tensor")
    d = lax.axis_index("dp")
    c = lax.rem(t, 2)
    y = lax.rem(t // 2, NY)
    zl = t // (2 * NY)
    x = lax.rem(d, NX)
    zh = d // NX
    z = 2 * zh + zl

    def dev(dx, yy, zz, cc):
        xx = lax.rem(x + dx + NX, NX)
        return {"tensor": (lax.rem(zz, 2) * NY + yy) * 2 + cc, "dp": (zz // 2) * NX + xx}

    def ring(v, off):
        return lax.rem(v + off + 4, 4)

    def frame(cc):
        return y + cc * (z - y), z + cc * (y - z)

    def slot(cc, uu, vv):
        yy, zz = uu + cc * (vv - uu), vv + cc * (uu - vv)
        return NZ * yy + zz

    def uv_dev(uu, vv):
        return dev(0, uu + c * (vv - uu), vv + c * (uu - vv), c)

    def at_rows(index, count=chip, offset=0):
        return pl.ds(pl.multiple_of(chip * index + offset, 16), count)

    partner = dev(0, y, z, 1 - c)
    right, left = dev(1, y, z, c), dev(-1, y, z, c)
    across = dev(0, y, ring(z, 2), c)
    pending = []

    def rcopy(src, dst, ss, rs, to):
        return pltpu.make_async_remote_copy(
            src_ref=src, dst_ref=dst, send_sem=ss, recv_sem=rs,
            device_id=to, device_id_type=pl.DeviceIdType.MESH,
        )

    def send(src, dst, ss, rs, to):
        copy = rcopy(src, dst, ss, rs, to)
        copy.start()
        pending.append(copy)
        return copy

    first = pl.ds(pl.multiple_of(zh * full, 128), full)
    shared = pl.ds(2 * full, pad - full)
    loads = [
        pltpu.make_async_copy(wg_hbm.at[:, first], wg.at[:, pl.ds(0, full)], w_sem.at[0]),
        pltpu.make_async_copy(wg_hbm.at[:, shared], wg.at[:, pl.ds(full, pad - full)], w_sem.at[1]),
        pltpu.make_async_copy(wu_hbm.at[:, first], wu.at[:, pl.ds(0, full)], w_sem.at[2]),
        pltpu.make_async_copy(wu_hbm.at[:, shared], wu.at[:, pl.ds(full, pad - full)], w_sem.at[3]),
        pltpu.make_async_copy(wd_hbm.at[first, :], wd.at[pl.ds(0, full), :], w_sem.at[4]),
        pltpu.make_async_copy(wd_hbm.at[shared, :], wd.at[pl.ds(full, pad - full), :], w_sem.at[5]),
    ]
    for load in loads:
        load.start()

    barrier = pltpu.get_barrier_semaphore()
    greeted = [partner, right, left]
    for ry in range(NY):
        for rz in range(NZ):
            if ry or rz:
                greeted.append(dev(0, ring(y, ry), ring(z, rz), c))
    for to in greeted:
        pl.semaphore_signal(barrier, inc=1, device_id=to, device_id_type=pl.DeviceIdType.MESH)

    me = NZ * y + z
    for a, src in enumerate((x_in, g_in)):
        xg[a, at_rows(me, main, main * c), :] = src[0:main, :]
        last = src[main:rows, :].astype(F32)
        none = jnp.zeros_like(last)
        tail[a] = jnp.concatenate(
            [jnp.where(c == 0, last, none), jnp.where(c == 0, none, last)], axis=0
        ).astype(BF16)
    pl.semaphore_wait(barrier, len(greeted))

    for a in range(2):
        mine = xg.at[a, at_rows(me, main, main * c), :]
        send(mine, mine, core_ss.at[a, 0], core_rs.at[a, 0], partner)
        send(tail.at[a], ptail.at[a], core_ss.at[a, 1], core_rs.at[a, 1], partner)

    u, v = frame(c)
    pu, pv = frame(1 - c)
    GROUPS = (0, -1, 1, 2)

    def columns(w, cc, part=None):
        slab, start, count = PARTS[w]
        size = count * quarter if part is None else count * quarter // 2
        col = start * quarter + cc * count * quarter + (0 if part is None else part * size)
        return pl.ds(pl.multiple_of(col, 512), size)

    def region(w, ou, ov, part=None):
        return xg.at[PARTS[w][0], at_rows(slot(c, ring(u, ou), ring(v, ov))), columns(w, c, part)]

    def partner_region(w, ou, ov):
        return xg.at[PARTS[w][0], at_rows(slot(1 - c, ring(pu, ou), ring(pv, ov))), columns(w, 1 - c)]

    def place(label):
        if label < 4:
            base, kind, axis = 0, label, 0
        else:
            base, kind, axis = GROUPS[(label - 4) // 4], label % 4, 1
        off = (-1, 1, 2, 2)[kind]
        part = (None, None, 0, 1)[kind]
        return (off, 0, part) if axis == 0 else (base, off, part)

    def arrived(a, label):
        where = region(a, *place(label))
        rcopy(where, where, ag_ss.at[a, label], ag_rs.at[a, label], partner).wait_recv()

    def pass_on(a, label, where, to):
        send(where, where, ag_ss.at[a, label], ag_rs.at[a, label], to)

    u_plus, u_minus = uv_dev(ring(u, 1), v), uv_dev(ring(u, -1), v)
    v_plus, v_minus = uv_dev(u, ring(v, 1)), uv_dev(u, ring(v, -1))

    def share(a, ou, ov):
        n = 4 * (ou % 4) + ov % 4
        where = region(a, ou, ov)
        send(where, where, sh_ss.at[a, n], sh_rs.at[a, n], partner)

    def along_v(a, r):
        where = region(a, GROUPS[r], 0)
        pass_on(a, 4 + 4 * r, where, v_plus)
        pass_on(a, 5 + 4 * r, where, v_minus)

    def gather_steps(a):
        def begin():
            if a < 2:
                mine = xg.at[a, at_rows(me, main, main * (1 - c)), :]
                rcopy(mine, mine, core_ss.at[a, 0], core_rs.at[a, 0], partner).wait_recv()
                rcopy(tail.at[a], ptail.at[a], core_ss.at[a, 1], core_rs.at[a, 1], partner).wait_recv()
                xg[a, at_rows(me, 2 * rest, 2 * main), :] = tail[a] + ptail[a]
            where = region(a, 0, 0)
            pass_on(a, 0, where, u_plus)
            pass_on(a, 1, where, u_minus)
            along_v(a, 0)

        def u_step(kind):
            off = (-1, 1)[kind]
            arrived(a, kind)
            pass_on(a, 2 + kind, region(a, off, 0, kind), (u_plus, u_minus)[kind])
            along_v(a, 1 + kind)
            share(a, off, 0)

        def u_last():
            arrived(a, 2)
            arrived(a, 3)
            along_v(a, 3)
            share(a, 2, 0)

        def v_step(r, kind):
            off = (-1, 1)[kind]
            arrived(a, 4 + 4 * r + kind)
            pass_on(a, 6 + 4 * r + kind, region(a, GROUPS[r], off, kind), (v_plus, v_minus)[kind])
            share(a, GROUPS[r], off)

        def v_last(r):
            arrived(a, 6 + 4 * r)
            arrived(a, 7 + 4 * r)
            share(a, GROUPS[r], 2)

        def take():
            for ou in range(4):
                for ov in range(4):
                    if ou or ov:
                        n = 4 * ou + ov
                        where = partner_region(a, ou, ov)
                        rcopy(where, where, sh_ss.at[a, n], sh_rs.at[a, n], partner).wait_recv()

        steps = [begin, functools.partial(u_step, 0), functools.partial(u_step, 1), u_last]
        for r in range(4):
            steps += [functools.partial(v_step, r, 0), functools.partial(v_step, r, 1)]
            if r:
                steps.append(functools.partial(v_last, r - 1))
        steps += [functools.partial(v_last, 3), take]
        return steps

    steps_x, steps_a, steps_b = gather_steps(0), gather_steps(1), gather_steps(2)

    def run(steps):
        for step in steps:
            step()

    run(steps_x[:4] + steps_a[:1] + steps_x[4:8] + steps_a[1:4] + steps_x[8:])
    later = steps_a[4:9] + steps_b[:1] + steps_a[9:]

    for load in loads[:4]:
        load.wait()
    piece = 256

    def put_transposed(which, n, span, value):
        turned = value.T
        if n == 0:
            lt[which, 0:piece, span] = turned
        else:
            keep = full - piece
            lt[which, piece:full, span] = turned[0:keep]
            side = hid - full
            lt[which, full:hid, span] = jnp.where(
                zh == 0, turned[keep:keep + side], turned[keep + side:keep + 2 * side]
            )

    def gate_piece(i, n):
        span = pl.ds(pl.multiple_of(i * piece, piece), piece)
        slab = xg[0, span, :]
        cols = pl.ds(n * piece, piece)
        gate = jnp.dot(slab, wg[:, cols], preferred_element_type=F32)
        up = jnp.dot(slab, wu[:, cols], preferred_element_type=F32)
        sig = jax.nn.sigmoid(gate)
        act = gate * sig
        fb[span, cols] = act.astype(BF16)
        fa[span, cols] = (up * sig * (1.0 + gate * (1.0 - sig))).astype(BF16)
        put_transposed(HIDDEN, n, span, (act * up).astype(BF16))

    pieces = tokens // piece
    done = 0
    for i in range(pieces):
        for n in range(2):
            gate_piece(i, n)
            until = len(later) * (2 * i + n + 1) // (2 * pieces)
            run(later[done:until])
            done = until

    def factors(j, xx):
        which, side = JOBS[j]
        side = (0, 1, 1 - zh, zh)[side]
        col = pl.multiple_of(side * half + lax.rem(xx, NX) * block, block)
        return jnp.dot(
            lt[which], xg[1 if which == HIDDEN else 0, :, pl.ds(col, block)],
            preferred_element_type=F32,
        )

    top, low = pl.ds(0, hid // 2), pl.ds(hid // 2, hid // 2)
    R, OPP, L = 0, 1, 2
    opposite = {}

    def multiply(j):
        def one(s, carry):
            own[j, s] = factors(j, x + 1 + s).astype(BF16)
            return carry

        def send_opposite():
            opposite[j] = [
                rcopy(own.at[j, OPP, top], fwd.at[j, 0], x_ss.at[j, 0], x_rs.at[j, 0], right),
                rcopy(own.at[j, OPP, low], fwd.at[j, 1], x_ss.at[j, 1], x_rs.at[j, 1], left),
            ]
            for copy in opposite[j]:
                copy.start()

        if j == 0:
            one(OPP, 0)
            send_opposite()
            one(R, 0)
            one(L, 0)
        else:
            lax.fori_loop(0, 3, one, 0)
            send_opposite()
        send(own.at[j, R, low], got.at[j, 0, low], x_ss.at[j, 2], x_rs.at[j, 2], right)
        send(own.at[j, L, top], got.at[j, 1, top], x_ss.at[j, 3], x_rs.at[j, 3], left)

    def add_on(j):
        for n, (s, part, to) in enumerate(((R, top, right), (L, low, left))):
            rcopy(fwd.at[j, n], fwd.at[j, n], x_ss.at[j, n], x_rs.at[j, n], partner).wait_recv()
            own[j, s, part] = (own[j, s, part].astype(F32) + fwd[j, n].astype(F32)).astype(BF16)
            send(own.at[j, s, part], got.at[j, n, part], x_ss.at[j, 4 + n], x_rs.at[j, 4 + n], to)

    out_rows = (
        (pl.ds(0, full), pl.ds(pl.multiple_of(zh * full, 64), full)),
        (pl.ds(full, hid - full), pl.ds(pl.multiple_of(2 * full + zh * (hid - full), 64), hid - full)),
    )
    in_rows = (
        pl.ds(pl.multiple_of((1 - zh) * full, 64), full),
        pl.ds(pl.multiple_of(2 * full + (1 - zh) * (hid - full), 64), hid - full),
    )
    outs = {HIDDEN: out_d, GATE: out_g, UP: out_u}
    local = []

    def prepare(j):
        for copy in opposite[j]:
            copy.wait_send()
        own[j, OPP] = factors(j, x).astype(BF16)

    def finish(j):
        which, side = JOBS[j]
        for n, (a, b) in enumerate(((top, low), (low, top))):
            rcopy(got.at[j, n, b], got.at[j, n, b], x_ss.at[j, 2 + n], x_rs.at[j, 2 + n], partner).wait_recv()
            rcopy(got.at[j, n, a], got.at[j, n, a], x_ss.at[j, 4 + n], x_rs.at[j, 4 + n], partner).wait_recv()
        total = own[j, OPP].astype(F32) + got[j, 0].astype(F32) + got[j, 1].astype(F32)
        own[j, OPP] = (total * scale).astype(BF16)
        for n, (here, there) in enumerate(out_rows):
            src, dst = own.at[j, OPP, here], outs[which].at[there, :]
            def away():
                return rcopy(src, dst, z_ss.at[which, n], z_rs.at[which, n], across)

            def stay():
                return pltpu.make_async_copy(src, dst, loc_sem.at[which, n])

            if side == OTHER:
                away().start()
            elif side == SAME:
                stay().start()
            else:
                pl.when(zh != side)(lambda: away().start())
                pl.when(zh == side)(lambda: stay().start())
            if side in (OTHER, LOW):
                pending.append(away())
            if side in (SAME, HIGH):
                local.append(stay())

    multiply(0)
    run(steps_b[1:10])
    add_on(0)
    run(steps_b[10:])
    multiply(1)

    loads[4].wait()
    loads[5].wait()

    def grad_piece(i, carry):
        span = pl.ds(pl.multiple_of(i * piece, piece), piece)
        slab = xg[1, span, :]
        for n in range(2):
            cols = pl.ds(n * piece, piece)
            back = nt(slab, wd[cols, :])
            gate_grad = (back * fa[span, cols].astype(F32)).astype(BF16)
            up_grad = (back * fb[span, cols].astype(F32)).astype(BF16)
            put_transposed(GATE, n, span, gate_grad)
            put_transposed(UP, n, span, up_grad)
            if n:
                lane = lax.broadcasted_iota(jnp.int32, (piece, piece), 1) - (full - piece)
                side = hid - full
                valid = (lane < 0) | ((lane >= side * zh) & (lane < side * (zh + 1)))
                gate_grad = jnp.where(valid, gate_grad, jnp.zeros_like(gate_grad))
                up_grad = jnp.where(valid, up_grad, jnp.zeros_like(up_grad))
            gu[0, span, cols] = gate_grad
            gu[1, span, cols] = up_grad
        return carry

    lax.fori_loop(0, pieces, grad_piece, 0)

    add_on(1)
    multiply(2)
    prepare(0)

    order = (2, 1, 3, 0)
    strip = 512
    strips = half // strip

    def back_piece(k, cc, add):
        buf = (fa, fb)[k % 2]
        uu, vv = frame(cc)
        spans = [at_rows(slot(cc, ring(uu, order[k]), ring(vv, rv))) for rv in range(4)]

        def one(n, carry):
            at = pl.ds(pl.multiple_of(cc * half + n * strip, strip), strip)
            held = pl.ds(pl.multiple_of(n * plane, 16), plane)
            value = sum(
                nt(jnp.concatenate([gu[w, span, :] for span in spans], axis=0), weight[at, :])
                for w, weight in enumerate((wg, wu))
            )
            if add:
                value += pst[k % 2, held, :].astype(F32)
                wd[0:plane, pl.ds(pl.multiple_of((k % 2) * half + n * strip, strip), strip)] = value.astype(BF16)
            else:
                buf[held, :] = value.astype(BF16)
            return carry

        lax.fori_loop(0, strips, one, 0)

    to_partner = []

    def give_piece(k):
        if k >= 2:
            to_partner[k - 2].wait_send()
        back_piece(k, 1 - c, False)
        copy = rcopy((fa, fb)[k % 2], p_hbm.at[k], p_ss.at[k], p_rs.at[k], partner)
        copy.start()
        to_partner.append(copy)

    def fetch(k):
        rcopy(p_hbm.at[k], p_hbm.at[k], p_ss.at[k], p_rs.at[k], partner).wait_recv()
        copy = pltpu.make_async_copy(p_hbm.at[k], pst.at[k % 2], fetch_sem.at[k % 2])
        copy.start()
        return copy

    def spread(k):
        for rv in (2, 1, 3):
            q = 3 * k + rv - 1
            src = s_hbm.at[k, pl.ds(chip * rv, chip), :]
            send(src, r_hbm.at[q], r_ss.at[q], r_rs.at[q], uv_dev(u, ring(v, rv)))

    written = []

    def sum_piece(k, fetched):
        fetched.wait()
        back_piece(k, c, True)
        copy = pltpu.make_async_copy(
            wd.at[pl.ds(0, plane), pl.ds((k % 2) * half, half)], s_hbm.at[k], fetch_sem.at[2 + k % 2]
        )
        copy.start()
        written.append(copy)

    def send_piece(k):
        written[k].wait()
        spread(k)

    give_piece(0)
    give_piece(1)
    finish(0)
    p0 = fetch(0)
    give_piece(2)
    sum_piece(0, p0)
    p1 = fetch(1)
    multiply(3)
    send_piece(0)
    sum_piece(1, p1)
    add_on(2)
    give_piece(3)
    send_piece(1)
    p2 = fetch(2)
    prepare(1)
    finish(1)
    p3 = fetch(3)
    sum_piece(2, p2)
    prepare(2)
    send_piece(2)
    sum_piece(3, p3)
    add_on(3)
    send_piece(3)
    multiply(4)
    multiply(5)
    to_partner[2].wait_send()
    to_partner[3].wait_send()
    finish(2)
    prepare(3)
    prepare(4)
    add_on(4)
    finish(3)

    def collect(arrivals, kept, k):
        places = [
            wd.at[pl.ds(chip * (n // 2 + 2 * (k % 2)), chip), pl.ds((n % 2) * half, half)] for n in range(4)
        ]
        copies = []
        for n, q in enumerate(arrivals):
            rcopy(r_hbm.at[q], r_hbm.at[q], r_ss.at[q], r_rs.at[q], partner).wait_recv()
            copies.append(pltpu.make_async_copy(r_hbm.at[q], places[n], fetch_sem.at[4 + n]))
        if kept is not None:
            copies.append(pltpu.make_async_copy(kept, places[3], fetch_sem.at[7]))
        for copy in copies:
            copy.start()
        for copy in copies:
            copy.wait()
        span = half // 4
        for n in range(4):
            at = pl.ds(n * span, span)
            terms = [place[:, at].astype(F32) for place in places[:len(copies)]]
            if kept is None:
                terms.append(sums[3, :, at].astype(F32))
            sums[k, :, at] = sum(terms).astype(BF16)

    for k in range(4):
        collect([3 * k, 3 * k + 1, 3 * k + 2], s_hbm.at[k, pl.ds(0, chip), :], k)
        r = order[k]
        if r:
            q = 11 + r
            send(sums.at[k], r_hbm.at[q], r_ss.at[q], r_rs.at[q], uv_dev(ring(u, r), v))
    prepare(5)
    add_on(5)
    collect([12, 13, 14], None, 4)

    mine = pl.ds(pl.multiple_of(c * half, half), half)
    theirs = pl.ds(pl.multiple_of((1 - c) * half, half), half)
    keep = sums.at[4, pl.ds(pl.multiple_of(main * c, 16), main), :]
    give = sums.at[4, pl.ds(pl.multiple_of(main * (1 - c), 16), main), :]
    ends = sums.at[4, pl.ds(2 * main, 2 * rest), :]
    send(give, ig_main.at[:, mine], o_ss.at[0], o_rs.at[0], partner)
    send(ends, ig_tail.at[:, mine], o_ss.at[1], o_rs.at[1], partner)
    for n, (src, dst) in enumerate(((keep, ig_main.at[:, mine]), (ends, ig_tail.at[:, mine]))):
        copy = pltpu.make_async_copy(src, dst, fetch_sem.at[n])
        copy.start()
        local.append(copy)

    finish(4)
    finish(5)

    for n, (src, dst) in enumerate(((keep, ig_main), (ends, ig_tail))):
        rcopy(src, dst.at[:, theirs], o_ss.at[n], o_rs.at[n], partner).wait_recv()
    for which in (HIDDEN, GATE, UP):
        for n, (here, _) in enumerate(out_rows):
            rcopy(own.at[0, OPP, here], outs[which].at[in_rows[n], :], z_ss.at[which, n], z_rs.at[which, n], partner).wait_recv()
    for copy in pending:
        copy.wait_send()
    for copy in local:
        copy.wait()


def arrange(gate_t, up_t, down, ig_main, ig_tail, grad_gate, grad_up, grad_down, input_grad):
    main = ig_main.shape[0]
    rest = input_grad.shape[0] - main
    core = lax.rem(lax.axis_index("tensor"), 2)
    ends = ig_tail[...].astype(F32)
    input_grad[0:main, :] = ig_main[...]
    input_grad[main:, :] = jnp.where(core == 0, ends[0:rest], ends[rest:]).astype(BF16)
    for n in range(gate_t.shape[0] // 128):
        at = pl.ds(n * 128, 128)
        grad_gate[:, at] = gate_t[at, :].T
        grad_up[:, at] = up_t[at, :].T
    grad_down[...] = down[...]


def local(inputs, out_grad, w_gate, w_up, w_down):
    _, rows, width = inputs.shape
    units = w_gate.shape[1]
    hid = units // 2
    pad = hid + 64
    tokens = 2 * rows * NY * NZ
    half = width // 2
    block = width // 8
    chip = 2 * rows
    scale = 1.0 / math.sqrt(rows * lax.axis_size("tensor") * lax.axis_size("dp"))
    dma = pltpu.SemaphoreType.DMA
    any_ = pl.BlockSpec(memory_space=pl.ANY)
    vmem = pl.BlockSpec(memory_space=pltpu.VMEM)
    arr = lambda *shape: jax.ShapeDtypeStruct(shape, BF16)
    outs = pl.pallas_call(
        functools.partial(kernel, scale),
        out_shape=(
            arr(units, block), arr(units, block), arr(units, block),
            arr(rows // 16 * 16, width), arr(16, width),
            arr(4, tokens, half // 4), arr(4, tokens // 4, half), arr(NY * NZ - 1, chip, half),
        ),
        in_specs=[vmem, vmem, any_, any_, any_],
        out_specs=(any_,) * 8,
        scratch_shapes=[
            pltpu.VMEM((2, tokens, width), BF16),
            pltpu.VMEM((width, pad), BF16),
            pltpu.VMEM((width, pad), BF16),
            pltpu.VMEM((pad, width), BF16),
            pltpu.VMEM((tokens, pad), BF16),
            pltpu.VMEM((tokens, pad), BF16),
            pltpu.VMEM((3, hid, tokens), BF16),
            pltpu.VMEM((2, tokens, pad), BF16),
            pltpu.VMEM((6, 3, hid, block), BF16),
            pltpu.VMEM((6, 2, hid // 2, block), BF16),
            pltpu.VMEM((6, 2, hid, block), BF16),
            pltpu.VMEM((5, chip, half), BF16),
            pltpu.VMEM((2, tokens, half // 4), BF16),
            pltpu.VMEM((2, 16, width), BF16),
            pltpu.VMEM((2, 16, width), BF16),
            dma((6,)), dma((2, 2)), dma((2, 2)),
            dma((3, 20)), dma((3, 20)), dma((3, 16)), dma((3, 16)),
            dma((6, 6)), dma((6, 6)),
            dma((4,)), dma((4,)), dma((15,)), dma((15,)),
            dma((3, 2)), dma((3, 2)), dma((2,)), dma((2,)),
            dma((3, 2)), dma((8,)),
        ],
        compiler_params=pltpu.CompilerParams(
            collective_id=0, has_side_effects=True, vmem_limit_bytes=63 * 2**20
        ),
        cost_estimate=pl.CostEstimate(
            flops=16 * tokens * width * hid, bytes_accessed=6 * width * units, transcendentals=tokens * hid
        ),
    )(inputs[0], out_grad[0], w_gate, w_up, w_down)
    grad_gate, grad_up, grad_down, input_grad = pl.pallas_call(
        arrange,
        out_shape=(arr(block, units), arr(block, units), arr(units, block), arr(rows, width)),
        in_specs=[vmem] * 5,
        out_specs=(vmem,) * 4,
    )(*outs[:5])
    return (input_grad[None], grad_gate, grad_up, grad_down)


def solution(mesh):
    placed = (
        P("dp", "tensor", None),
        P("dp", "tensor", None),
        P(None, "tensor"),
        P(None, "tensor"),
        P("tensor", None),
    )
    return jax.shard_map(
        local,
        mesh=mesh,
        in_specs=placed,
        out_specs=(
            P("dp", "tensor", None),
            P("dp", "tensor"),
            P("dp", "tensor"),
            P("tensor", "dp"),
        ),
        check_vma=False,
    )
```

```python
import functools
import math

import jax
import jax.numpy as jnp
from jax import lax
from jax.experimental import pallas as pl
from jax.experimental.pallas import tpu as pltpu
from jax.sharding import PartitionSpec as P

BF16 = jnp.bfloat16
F32 = jnp.float32
NX = NY = NZ = 4
NT = (((1,), (1,)), ((), ()))
HIDDEN, GATE, UP = 0, 1, 2
LOW, HIGH, OTHER, SAME = 0, 1, 2, 3
JOBS = ((HIDDEN, LOW), (HIDDEN, HIGH), (GATE, OTHER), (UP, OTHER), (GATE, SAME), (UP, SAME))
PARTS = ((0, 0, 2), (1, 0, 1), (1, 2, 1))


def nt(left, right):
    return lax.dot_general(left, right, NT, preferred_element_type=F32)


def kernel(
    scale, x_in, g_in, wg_hbm, wu_hbm, wd_hbm,
    out_g, out_u, out_d, ig_main, ig_tail, p_hbm, s_hbm, r_hbm,
    xg, wg, wu, wd, fa, fb, lt, gu, own, fwd, got, sums, pst, tail, ptail,
    w_sem, core_ss, core_rs, ag_ss, ag_rs, sh_ss, sh_rs, x_ss, x_rs,
    p_ss, p_rs, r_ss, r_rs, z_ss, z_rs, o_ss, o_rs, loc_sem, fetch_sem,
):
    rows, width = x_in.shape
    half = width // 2
    quarter = half // 2
    main = rows // 16 * 16
    rest = rows - main
    chip = 2 * rows
    tokens = xg.shape[1]
    plane = NZ * chip
    hid = lt.shape[1]
    pad = wg.shape[1]
    full = pad - 128
    block = width // 8

    t = lax.axis_index("tensor")
    d = lax.axis_index("dp")
    c = lax.rem(t, 2)
    y = lax.rem(t // 2, NY)
    zl = t // (2 * NY)
    x = lax.rem(d, NX)
    zh = d // NX
    z = 2 * zh + zl

    def dev(dx, yy, zz, cc):
        xx = lax.rem(x + dx + NX, NX)
        return {"tensor": (lax.rem(zz, 2) * NY + yy) * 2 + cc, "dp": (zz // 2) * NX + xx}

    def ring(v, off):
        return lax.rem(v + off + 4, 4)

    def frame(cc):
        return y + cc * (z - y), z + cc * (y - z)

    def slot(cc, uu, vv):
        yy, zz = uu + cc * (vv - uu), vv + cc * (uu - vv)
        return NZ * yy + zz

    def uv_dev(uu, vv):
        return dev(0, uu + c * (vv - uu), vv + c * (uu - vv), c)

    def at_rows(index, count=chip, offset=0):
        return pl.ds(pl.multiple_of(chip * index + offset, 16), count)

    partner = dev(0, y, z, 1 - c)
    right, left = dev(1, y, z, c), dev(-1, y, z, c)
    across = dev(0, y, ring(z, 2), c)
    pending = []

    def rcopy(src, dst, ss, rs, to):
        return pltpu.make_async_remote_copy(
            src_ref=src, dst_ref=dst, send_sem=ss, recv_sem=rs,
            device_id=to, device_id_type=pl.DeviceIdType.MESH,
        )

    def send(src, dst, ss, rs, to):
        copy = rcopy(src, dst, ss, rs, to)
        copy.start()
        pending.append(copy)
        return copy

    first = pl.ds(pl.multiple_of(zh * full, 128), full)
    shared = pl.ds(2 * full, pad - full)
    loads = [
        pltpu.make_async_copy(wg_hbm.at[:, first], wg.at[:, pl.ds(0, full)], w_sem.at[0]),
        pltpu.make_async_copy(wg_hbm.at[:, shared], wg.at[:, pl.ds(full, pad - full)], w_sem.at[1]),
        pltpu.make_async_copy(wu_hbm.at[:, first], wu.at[:, pl.ds(0, full)], w_sem.at[2]),
        pltpu.make_async_copy(wu_hbm.at[:, shared], wu.at[:, pl.ds(full, pad - full)], w_sem.at[3]),
        pltpu.make_async_copy(wd_hbm.at[first, :], wd.at[pl.ds(0, full), :], w_sem.at[4]),
        pltpu.make_async_copy(wd_hbm.at[shared, :], wd.at[pl.ds(full, pad - full), :], w_sem.at[5]),
    ]
    for load in loads:
        load.start()

    barrier = pltpu.get_barrier_semaphore()
    greeted = [partner, right, left]
    for ry in range(NY):
        for rz in range(NZ):
            if ry or rz:
                greeted.append(dev(0, ring(y, ry), ring(z, rz), c))
    for to in greeted:
        pl.semaphore_signal(barrier, inc=1, device_id=to, device_id_type=pl.DeviceIdType.MESH)

    me = NZ * y + z
    for a, src in enumerate((x_in, g_in)):
        xg[a, at_rows(me, main, main * c), :] = src[0:main, :]
        last = src[main:rows, :].astype(F32)
        none = jnp.zeros_like(last)
        tail[a] = jnp.concatenate(
            [jnp.where(c == 0, last, none), jnp.where(c == 0, none, last)], axis=0
        ).astype(BF16)
    pl.semaphore_wait(barrier, len(greeted))

    for a in range(2):
        mine = xg.at[a, at_rows(me, main, main * c), :]
        send(mine, mine, core_ss.at[a, 0], core_rs.at[a, 0], partner)
        send(tail.at[a], ptail.at[a], core_ss.at[a, 1], core_rs.at[a, 1], partner)

    u, v = frame(c)
    pu, pv = frame(1 - c)
    GROUPS = (0, -1, 1, 2)

    def columns(w, cc, part=None):
        slab, start, count = PARTS[w]
        size = count * quarter if part is None else count * quarter // 2
        col = start * quarter + cc * count * quarter + (0 if part is None else part * size)
        return pl.ds(pl.multiple_of(col, 512), size)

    def region(w, ou, ov, part=None):
        return xg.at[PARTS[w][0], at_rows(slot(c, ring(u, ou), ring(v, ov))), columns(w, c, part)]

    def partner_region(w, ou, ov):
        return xg.at[PARTS[w][0], at_rows(slot(1 - c, ring(pu, ou), ring(pv, ov))), columns(w, 1 - c)]

    def place(label):
        if label < 4:
            base, kind, axis = 0, label, 0
        else:
            base, kind, axis = GROUPS[(label - 4) // 4], label % 4, 1
        off = (-1, 1, 2, 2)[kind]
        part = (None, None, 0, 1)[kind]
        return (off, 0, part) if axis == 0 else (base, off, part)

    def arrived(a, label):
        where = region(a, *place(label))
        rcopy(where, where, ag_ss.at[a, label], ag_rs.at[a, label], partner).wait_recv()

    def pass_on(a, label, where, to):
        send(where, where, ag_ss.at[a, label], ag_rs.at[a, label], to)

    u_plus, u_minus = uv_dev(ring(u, 1), v), uv_dev(ring(u, -1), v)
    v_plus, v_minus = uv_dev(u, ring(v, 1)), uv_dev(u, ring(v, -1))

    def share(a, ou, ov):
        n = 4 * (ou % 4) + ov % 4
        where = region(a, ou, ov)
        send(where, where, sh_ss.at[a, n], sh_rs.at[a, n], partner)

    def along_v(a, r):
        where = region(a, GROUPS[r], 0)
        pass_on(a, 4 + 4 * r, where, v_plus)
        pass_on(a, 5 + 4 * r, where, v_minus)

    def gather_steps(a):
        def begin():
            if a < 2:
                mine = xg.at[a, at_rows(me, main, main * (1 - c)), :]
                rcopy(mine, mine, core_ss.at[a, 0], core_rs.at[a, 0], partner).wait_recv()
                rcopy(tail.at[a], ptail.at[a], core_ss.at[a, 1], core_rs.at[a, 1], partner).wait_recv()
                xg[a, at_rows(me, 2 * rest, 2 * main), :] = tail[a] + ptail[a]
            where = region(a, 0, 0)
            pass_on(a, 0, where, u_plus)
            pass_on(a, 1, where, u_minus)
            along_v(a, 0)

        def u_step(kind):
            off = (-1, 1)[kind]
            arrived(a, kind)
            pass_on(a, 2 + kind, region(a, off, 0, kind), (u_plus, u_minus)[kind])
            along_v(a, 1 + kind)
            share(a, off, 0)

        def u_last():
            arrived(a, 2)
            arrived(a, 3)
            along_v(a, 3)
            share(a, 2, 0)

        def v_step(r, kind):
            off = (-1, 1)[kind]
            arrived(a, 4 + 4 * r + kind)
            pass_on(a, 6 + 4 * r + kind, region(a, GROUPS[r], off, kind), (v_plus, v_minus)[kind])
            share(a, GROUPS[r], off)

        def v_last(r):
            arrived(a, 6 + 4 * r)
            arrived(a, 7 + 4 * r)
            share(a, GROUPS[r], 2)

        def take():
            for ou in range(4):
                for ov in range(4):
                    if ou or ov:
                        n = 4 * ou + ov
                        where = partner_region(a, ou, ov)
                        rcopy(where, where, sh_ss.at[a, n], sh_rs.at[a, n], partner).wait_recv()

        steps = {"begin": begin, "u0": functools.partial(u_step, 0), "u1": functools.partial(u_step, 1)}
        steps.update(ulast=u_last, take=take)
        for r in range(4):
            for kind in range(2):
                steps[f"v{r}{kind}"] = functools.partial(v_step, r, kind)
            steps[f"vl{r}"] = functools.partial(v_last, r)
        return steps

    steps = [gather_steps(w) for w in range(len(PARTS))]

    def go(w, *names):
        for name in names:
            steps[w][name]()

    go(0, "begin", "u0", "u1", "v00", "v01", "ulast", "v10", "v11", "v20", "v21", "vl0", "v30", "v31", "vl1", "vl2")
    go(1, "begin")
    go(0, "vl3", "take")

    for load in loads[:4]:
        load.wait()
    piece = 256

    def put_transposed(which, n, span, value):
        turned = value.T
        if n == 0:
            lt[which, 0:piece, span] = turned
        else:
            keep = full - piece
            lt[which, piece:full, span] = turned[0:keep]
            side = hid - full
            lt[which, full:hid, span] = jnp.where(
                zh == 0, turned[keep:keep + side], turned[keep + side:keep + 2 * side]
            )

    def gate_piece(i, n):
        span = pl.ds(pl.multiple_of(i * piece, piece), piece)
        slab = xg[0, span, :]
        cols = pl.ds(n * piece, piece)
        gate = jnp.dot(slab, wg[:, cols], preferred_element_type=F32)
        up = jnp.dot(slab, wu[:, cols], preferred_element_type=F32)
        sig = jax.nn.sigmoid(gate)
        act = gate * sig
        fb[span, cols] = act.astype(BF16)
        fa[span, cols] = (up * sig * (1.0 + gate * (1.0 - sig))).astype(BF16)
        put_transposed(HIDDEN, n, span, (act * up).astype(BF16))

    pieces = tokens // piece
    gates = [(i, n) for i in range(pieces) for n in range(2)]

    def gate(count):
        for _ in range(count):
            gate_piece(*gates.pop(0))

    gate(2)
    go(1, "u0", "u1", "v00", "v01")
    gate(2)
    go(1, "ulast", "v10", "v11")
    go(2, "begin")
    gate(1)
    go(1, "v20", "v21", "vl0")
    gate(2)
    go(1, "v30", "v31")
    go(2, "u0")
    go(1, "vl1")
    go(2, "u1")
    gate(1)
    go(2, "v00", "v01")
    gate(1)
    go(1, "vl2", "vl3")
    go(2, "ulast")
    gate(len(gates))
    go(2, "v10", "v11")
    go(1, "take")

    def factors(j, xx):
        which, side = JOBS[j]
        side = (0, 1, 1 - zh, zh)[side]
        col = pl.multiple_of(side * half + lax.rem(xx, NX) * block, block)
        return jnp.dot(
            lt[which], xg[1 if which == HIDDEN else 0, :, pl.ds(col, block)],
            preferred_element_type=F32,
        )

    top, low = pl.ds(0, hid // 2), pl.ds(hid // 2, hid // 2)
    R, OPP, L = 0, 1, 2
    opposite = {}

    def multiply_one(j, s):
        own[j, s] = factors(j, x + 1 + s).astype(BF16)

    def send_one(j, s):
        if s == OPP:
            opposite[j] = [
                rcopy(own.at[j, OPP, top], fwd.at[j, 0], x_ss.at[j, 0], x_rs.at[j, 0], right),
                rcopy(own.at[j, OPP, low], fwd.at[j, 1], x_ss.at[j, 1], x_rs.at[j, 1], left),
            ]
            for copy in opposite[j]:
                copy.start()
        elif s == R:
            send(own.at[j, R, low], got.at[j, 0, low], x_ss.at[j, 2], x_rs.at[j, 2], right)
        else:
            send(own.at[j, L, top], got.at[j, 1, top], x_ss.at[j, 3], x_rs.at[j, 3], left)

    def multiply(j):
        def one(s, carry):
            multiply_one(j, s)
            return carry

        lax.fori_loop(0, 3, one, 0)
        for s in (OPP, R, L):
            send_one(j, s)

    def add_on(j):
        for n, (s, part, to) in enumerate(((R, top, right), (L, low, left))):
            rcopy(fwd.at[j, n], fwd.at[j, n], x_ss.at[j, n], x_rs.at[j, n], partner).wait_recv()
            own[j, s, part] = (own[j, s, part].astype(F32) + fwd[j, n].astype(F32)).astype(BF16)
            send(own.at[j, s, part], got.at[j, n, part], x_ss.at[j, 4 + n], x_rs.at[j, 4 + n], to)

    out_rows = (
        (pl.ds(0, full), pl.ds(pl.multiple_of(zh * full, 64), full)),
        (pl.ds(full, hid - full), pl.ds(pl.multiple_of(2 * full + zh * (hid - full), 64), hid - full)),
    )
    in_rows = (
        pl.ds(pl.multiple_of((1 - zh) * full, 64), full),
        pl.ds(pl.multiple_of(2 * full + (1 - zh) * (hid - full), 64), hid - full),
    )
    outs = {HIDDEN: out_d, GATE: out_g, UP: out_u}
    local = []

    def prepare(j):
        for copy in opposite[j]:
            copy.wait_send()
        own[j, OPP] = factors(j, x).astype(BF16)

    def finish(j):
        which, side = JOBS[j]
        for n, (a, b) in enumerate(((top, low), (low, top))):
            rcopy(got.at[j, n, b], got.at[j, n, b], x_ss.at[j, 2 + n], x_rs.at[j, 2 + n], partner).wait_recv()
            rcopy(got.at[j, n, a], got.at[j, n, a], x_ss.at[j, 4 + n], x_rs.at[j, 4 + n], partner).wait_recv()
        total = own[j, OPP].astype(F32) + got[j, 0].astype(F32) + got[j, 1].astype(F32)
        own[j, OPP] = (total * scale).astype(BF16)
        for n, (here, there) in enumerate(out_rows):
            src, dst = own.at[j, OPP, here], outs[which].at[there, :]
            def away():
                return rcopy(src, dst, z_ss.at[which, n], z_rs.at[which, n], across)

            def stay():
                return pltpu.make_async_copy(src, dst, loc_sem.at[which, n])

            if side == OTHER:
                away().start()
            elif side == SAME:
                stay().start()
            else:
                pl.when(zh != side)(lambda: away().start())
                pl.when(zh == side)(lambda: stay().start())
            if side in (OTHER, LOW):
                pending.append(away())
            if side in (SAME, HIGH):
                local.append(stay())

    multiply_one(0, OPP)
    send_one(0, OPP)
    go(2, "v20", "v21")
    multiply_one(0, R)
    send_one(0, R)
    go(2, "vl0")
    multiply_one(0, L)
    send_one(0, L)
    go(2, "v30", "v31", "vl1", "vl2", "vl3", "take")
    add_on(0)
    for s in (OPP, R, L):
        multiply_one(1, s)
        send_one(1, s)

    loads[4].wait()
    loads[5].wait()

    def grad_piece(i, carry):
        span = pl.ds(pl.multiple_of(i * piece, piece), piece)
        slab = xg[1, span, :]
        for n in range(2):
            cols = pl.ds(n * piece, piece)
            back = nt(slab, wd[cols, :])
            gate_grad = (back * fa[span, cols].astype(F32)).astype(BF16)
            up_grad = (back * fb[span, cols].astype(F32)).astype(BF16)
            put_transposed(GATE, n, span, gate_grad)
            put_transposed(UP, n, span, up_grad)
            if n:
                lane = lax.broadcasted_iota(jnp.int32, (piece, piece), 1) - (full - piece)
                side = hid - full
                valid = (lane < 0) | ((lane >= side * zh) & (lane < side * (zh + 1)))
                gate_grad = jnp.where(valid, gate_grad, jnp.zeros_like(gate_grad))
                up_grad = jnp.where(valid, up_grad, jnp.zeros_like(up_grad))
            gu[0, span, cols] = gate_grad
            gu[1, span, cols] = up_grad
        return carry

    lax.fori_loop(0, pieces, grad_piece, 0)

    add_on(1)
    multiply(2)
    prepare(0)

    order = (2, 1, 3, 0)
    strip = 512
    strips = half // strip

    def back_piece(k, cc, add):
        buf = (fa, fb)[k % 2]
        uu, vv = frame(cc)
        spans = [at_rows(slot(cc, ring(uu, order[k]), ring(vv, rv))) for rv in range(4)]

        def one(n, carry):
            at = pl.ds(pl.multiple_of(cc * half + n * strip, strip), strip)
            held = pl.ds(pl.multiple_of(n * plane, 16), plane)
            value = sum(
                nt(jnp.concatenate([gu[w, span, :] for span in spans], axis=0), weight[at, :])
                for w, weight in enumerate((wg, wu))
            )
            if add:
                value += pst[k % 2, held, :].astype(F32)
                wd[0:plane, pl.ds(pl.multiple_of((k % 2) * half + n * strip, strip), strip)] = value.astype(BF16)
            else:
                buf[held, :] = value.astype(BF16)
            return carry

        lax.fori_loop(0, strips, one, 0)

    to_partner = []

    def give_piece(k):
        if k >= 2:
            to_partner[k - 2].wait_send()
        back_piece(k, 1 - c, False)
        copy = rcopy((fa, fb)[k % 2], p_hbm.at[k], p_ss.at[k], p_rs.at[k], partner)
        copy.start()
        to_partner.append(copy)

    def fetch(k):
        rcopy(p_hbm.at[k], p_hbm.at[k], p_ss.at[k], p_rs.at[k], partner).wait_recv()
        copy = pltpu.make_async_copy(p_hbm.at[k], pst.at[k % 2], fetch_sem.at[k % 2])
        copy.start()
        return copy

    def spread(k):
        for rv in (2, 1, 3):
            q = 3 * k + rv - 1
            src = s_hbm.at[k, pl.ds(chip * rv, chip), :]
            send(src, r_hbm.at[q], r_ss.at[q], r_rs.at[q], uv_dev(u, ring(v, rv)))

    written = []

    def sum_piece(k, fetched):
        fetched.wait()
        back_piece(k, c, True)
        copy = pltpu.make_async_copy(
            wd.at[pl.ds(0, plane), pl.ds((k % 2) * half, half)], s_hbm.at[k], fetch_sem.at[2 + k % 2]
        )
        copy.start()
        written.append(copy)

    def send_piece(k):
        written[k].wait()
        spread(k)

    give_piece(0)
    give_piece(1)
    finish(0)
    p0 = fetch(0)
    give_piece(2)
    sum_piece(0, p0)
    p1 = fetch(1)
    multiply(3)
    send_piece(0)
    sum_piece(1, p1)
    add_on(2)
    give_piece(3)
    send_piece(1)
    p2 = fetch(2)
    prepare(1)
    finish(1)
    p3 = fetch(3)
    sum_piece(2, p2)
    prepare(2)
    send_piece(2)
    sum_piece(3, p3)
    add_on(3)
    send_piece(3)
    multiply(4)
    multiply(5)
    to_partner[2].wait_send()
    to_partner[3].wait_send()
    finish(2)
    prepare(3)
    prepare(4)
    add_on(4)
    finish(3)

    def collect(arrivals, kept, k):
        places = [
            wd.at[pl.ds(chip * (n // 2 + 2 * (k % 2)), chip), pl.ds((n % 2) * half, half)] for n in range(4)
        ]
        copies = []
        for n, q in enumerate(arrivals):
            rcopy(r_hbm.at[q], r_hbm.at[q], r_ss.at[q], r_rs.at[q], partner).wait_recv()
            copies.append(pltpu.make_async_copy(r_hbm.at[q], places[n], fetch_sem.at[4 + n]))
        if kept is not None:
            copies.append(pltpu.make_async_copy(kept, places[3], fetch_sem.at[7]))
        for copy in copies:
            copy.start()
        for copy in copies:
            copy.wait()
        span = half // 4
        for n in range(4):
            at = pl.ds(n * span, span)
            terms = [place[:, at].astype(F32) for place in places[:len(copies)]]
            if kept is None:
                terms.append(sums[3, :, at].astype(F32))
            sums[k, :, at] = sum(terms).astype(BF16)

    for k in range(4):
        collect([3 * k, 3 * k + 1, 3 * k + 2], s_hbm.at[k, pl.ds(0, chip), :], k)
        r = order[k]
        if r:
            q = 11 + r
            send(sums.at[k], r_hbm.at[q], r_ss.at[q], r_rs.at[q], uv_dev(ring(u, r), v))
    prepare(5)
    add_on(5)
    collect([12, 13, 14], None, 4)

    mine = pl.ds(pl.multiple_of(c * half, half), half)
    theirs = pl.ds(pl.multiple_of((1 - c) * half, half), half)
    keep = sums.at[4, pl.ds(pl.multiple_of(main * c, 16), main), :]
    give = sums.at[4, pl.ds(pl.multiple_of(main * (1 - c), 16), main), :]
    ends = sums.at[4, pl.ds(2 * main, 2 * rest), :]
    send(give, ig_main.at[:, mine], o_ss.at[0], o_rs.at[0], partner)
    send(ends, ig_tail.at[:, mine], o_ss.at[1], o_rs.at[1], partner)
    for n, (src, dst) in enumerate(((keep, ig_main.at[:, mine]), (ends, ig_tail.at[:, mine]))):
        copy = pltpu.make_async_copy(src, dst, fetch_sem.at[n])
        copy.start()
        local.append(copy)

    finish(4)
    finish(5)

    for n, (src, dst) in enumerate(((keep, ig_main), (ends, ig_tail))):
        rcopy(src, dst.at[:, theirs], o_ss.at[n], o_rs.at[n], partner).wait_recv()
    for which in (HIDDEN, GATE, UP):
        for n, (here, _) in enumerate(out_rows):
            rcopy(own.at[0, OPP, here], outs[which].at[in_rows[n], :], z_ss.at[which, n], z_rs.at[which, n], partner).wait_recv()
    for copy in pending:
        copy.wait_send()
    for copy in local:
        copy.wait()


def arrange(
    gate_t, up_t, down, ig_main, ig_tail, grad_gate, grad_up, grad_down, input_grad,
    vg, vu, vd, vt, tg, tu, vi, sem,
):
    main = ig_main.shape[0]
    rest = input_grad.shape[0] - main
    core = lax.rem(lax.axis_index("tensor"), 2)
    moves = [
        pltpu.make_async_copy(src, dst, sem.at[n])
        for n, (src, dst) in enumerate(
            ((gate_t, vg), (up_t, vu), (down, vd), (ig_main, vi.at[pl.ds(0, main), :]), (ig_tail, vt))
        )
    ]
    backs = [
        pltpu.make_async_copy(src, dst, sem.at[5 + n])
        for n, (src, dst) in enumerate(((tg, grad_gate), (tu, grad_up), (vd, grad_down), (vi, input_grad)))
    ]
    for move in moves:
        move.start()
    for n, (src, dst) in enumerate(((vg, tg), (vu, tu))):
        moves[n].wait()
        for k in range(src.shape[0] // 128):
            at = pl.ds(k * 128, 128)
            dst[:, at] = src[at, :].T
        backs[n].start()
    moves[2].wait()
    backs[2].start()
    moves[3].wait()
    moves[4].wait()
    ends = vt[...].astype(F32)
    vi[main:, :] = jnp.where(core == 0, ends[0:rest], ends[rest:]).astype(BF16)
    backs[3].start()
    for back in backs:
        back.wait()


def local(inputs, out_grad, w_gate, w_up, w_down):
    _, rows, width = inputs.shape
    units = w_gate.shape[1]
    hid = units // 2
    pad = hid + 64
    tokens = 2 * rows * NY * NZ
    half = width // 2
    block = width // 8
    chip = 2 * rows
    scale = 1.0 / math.sqrt(rows * lax.axis_size("tensor") * lax.axis_size("dp"))
    dma = pltpu.SemaphoreType.DMA
    any_ = pl.BlockSpec(memory_space=pl.ANY)
    vmem = pl.BlockSpec(memory_space=pltpu.VMEM)
    arr = lambda *shape: jax.ShapeDtypeStruct(shape, BF16)
    outs = pl.pallas_call(
        functools.partial(kernel, scale),
        out_shape=(
            arr(units, block), arr(units, block), arr(units, block),
            arr(rows // 16 * 16, width), arr(16, width),
            arr(4, tokens, half // 4), arr(4, tokens // 4, half), arr(NY * NZ - 1, chip, half),
        ),
        in_specs=[vmem, vmem, any_, any_, any_],
        out_specs=(any_,) * 8,
        scratch_shapes=[
            pltpu.VMEM((2, tokens, width), BF16),
            pltpu.VMEM((width, pad), BF16),
            pltpu.VMEM((width, pad), BF16),
            pltpu.VMEM((pad, width), BF16),
            pltpu.VMEM((tokens, pad), BF16),
            pltpu.VMEM((tokens, pad), BF16),
            pltpu.VMEM((3, hid, tokens), BF16),
            pltpu.VMEM((2, tokens, pad), BF16),
            pltpu.VMEM((6, 3, hid, block), BF16),
            pltpu.VMEM((6, 2, hid // 2, block), BF16),
            pltpu.VMEM((6, 2, hid, block), BF16),
            pltpu.VMEM((5, chip, half), BF16),
            pltpu.VMEM((2, tokens, half // 4), BF16),
            pltpu.VMEM((2, 16, width), BF16),
            pltpu.VMEM((2, 16, width), BF16),
            dma((6,)), dma((2, 2)), dma((2, 2)),
            dma((3, 20)), dma((3, 20)), dma((3, 16)), dma((3, 16)),
            dma((6, 6)), dma((6, 6)),
            dma((4,)), dma((4,)), dma((15,)), dma((15,)),
            dma((3, 2)), dma((3, 2)), dma((2,)), dma((2,)),
            dma((3, 2)), dma((8,)),
        ],
        compiler_params=pltpu.CompilerParams(
            collective_id=0, has_side_effects=True, vmem_limit_bytes=63 * 2**20
        ),
        cost_estimate=pl.CostEstimate(
            flops=16 * tokens * width * hid, bytes_accessed=6 * width * units, transcendentals=tokens * hid
        ),
    )(inputs[0], out_grad[0], w_gate, w_up, w_down)
    grad_gate, grad_up, grad_down, input_grad = pl.pallas_call(
        arrange,
        out_shape=(arr(block, units), arr(block, units), arr(units, block), arr(rows, width)),
        in_specs=[any_] * 5,
        out_specs=(any_,) * 4,
        scratch_shapes=[
            pltpu.VMEM((units, block), BF16), pltpu.VMEM((units, block), BF16), pltpu.VMEM((units, block), BF16),
            pltpu.VMEM((16, width), BF16), pltpu.VMEM((block, units), BF16), pltpu.VMEM((block, units), BF16),
            pltpu.VMEM((rows, width), BF16), dma((9,)),
        ],
    )(*outs[:5])
    return (input_grad[None], grad_gate, grad_up, grad_down)


def solution(mesh):
    placed = (
        P("dp", "tensor", None),
        P("dp", "tensor", None),
        P(None, "tensor"),
        P(None, "tensor"),
        P("tensor", None),
    )
    return jax.shard_map(
        local,
        mesh=mesh,
        in_specs=placed,
        out_specs=(
            P("dp", "tensor", None),
            P("dp", "tensor"),
            P("dp", "tensor"),
            P("tensor", "dp"),
        ),
        check_vma=False,
    )
```

```python
import functools
import math

import jax
import jax.numpy as jnp
from jax import lax
from jax.experimental import pallas as pl
from jax.experimental.pallas import tpu as pltpu
from jax.sharding import PartitionSpec as P

BF16 = jnp.bfloat16
F32 = jnp.float32
NX = NY = NZ = 4
NT = (((1,), (1,)), ((), ()))
HIDDEN, GATE, UP = 0, 1, 2
LOW, HIGH, OTHER, SAME = 0, 1, 2, 3
JOBS = ((HIDDEN, LOW), (HIDDEN, HIGH), (GATE, OTHER), (UP, OTHER), (GATE, SAME), (UP, SAME))
PARTS = ((0, 0, 2), (1, 0, 1), (1, 2, 1))


def nt(left, right):
    return lax.dot_general(left, right, NT, preferred_element_type=F32)


def kernel(
    scale, x_in, g_in, wg_hbm, wu_hbm, wd_hbm,
    out_g, out_u, out_d, ig_main, ig_tail, p_hbm, s_hbm, r_hbm,
    xg, wg, wu, wd, fa, fb, lt, gu, own, fwd, got, sums, pst, tail, ptail,
    w_sem, core_ss, core_rs, ag_ss, ag_rs, sh_ss, sh_rs, x_ss, x_rs,
    p_ss, p_rs, r_ss, r_rs, z_ss, z_rs, o_ss, o_rs, loc_sem, fetch_sem,
):
    rows, width = x_in.shape
    half = width // 2
    quarter = half // 2
    main = rows // 16 * 16
    rest = rows - main
    chip = 2 * rows
    tokens = xg.shape[1]
    plane = NZ * chip
    hid = lt.shape[1]
    pad = wg.shape[1]
    full = pad - 128
    block = width // 8

    t = lax.axis_index("tensor")
    d = lax.axis_index("dp")
    c = lax.rem(t, 2)
    y = lax.rem(t // 2, NY)
    zl = t // (2 * NY)
    x = lax.rem(d, NX)
    zh = d // NX
    z = 2 * zh + zl

    def dev(dx, yy, zz, cc):
        xx = lax.rem(x + dx + NX, NX)
        return {"tensor": (lax.rem(zz, 2) * NY + yy) * 2 + cc, "dp": (zz // 2) * NX + xx}

    def ring(v, off):
        return lax.rem(v + off + 4, 4)

    def frame(cc):
        return y + cc * (z - y), z + cc * (y - z)

    def slot(cc, uu, vv):
        yy, zz = uu + cc * (vv - uu), vv + cc * (uu - vv)
        return NZ * yy + zz

    def uv_dev(uu, vv):
        return dev(0, uu + c * (vv - uu), vv + c * (uu - vv), c)

    def at_rows(index, count=chip, offset=0):
        return pl.ds(pl.multiple_of(chip * index + offset, 16), count)

    partner = dev(0, y, z, 1 - c)
    right, left = dev(1, y, z, c), dev(-1, y, z, c)
    across = dev(0, y, ring(z, 2), c)
    pending = []

    def rcopy(src, dst, ss, rs, to):
        return pltpu.make_async_remote_copy(
            src_ref=src, dst_ref=dst, send_sem=ss, recv_sem=rs,
            device_id=to, device_id_type=pl.DeviceIdType.MESH,
        )

    def send(src, dst, ss, rs, to):
        copy = rcopy(src, dst, ss, rs, to)
        copy.start()
        pending.append(copy)
        return copy

    first = pl.ds(pl.multiple_of(zh * full, 128), full)
    shared = pl.ds(2 * full, pad - full)
    loads = [
        pltpu.make_async_copy(wg_hbm.at[:, first], wg.at[:, pl.ds(0, full)], w_sem.at[0]),
        pltpu.make_async_copy(wg_hbm.at[:, shared], wg.at[:, pl.ds(full, pad - full)], w_sem.at[1]),
        pltpu.make_async_copy(wu_hbm.at[:, first], wu.at[:, pl.ds(0, full)], w_sem.at[2]),
        pltpu.make_async_copy(wu_hbm.at[:, shared], wu.at[:, pl.ds(full, pad - full)], w_sem.at[3]),
        pltpu.make_async_copy(wd_hbm.at[first, :], wd.at[pl.ds(0, full), :], w_sem.at[4]),
        pltpu.make_async_copy(wd_hbm.at[shared, :], wd.at[pl.ds(full, pad - full), :], w_sem.at[5]),
    ]
    for load in loads:
        load.start()

    barrier = pltpu.get_barrier_semaphore()
    greeted = [partner, right, left]
    for ry in range(NY):
        for rz in range(NZ):
            if ry or rz:
                greeted.append(dev(0, ring(y, ry), ring(z, rz), c))
    for to in greeted:
        pl.semaphore_signal(barrier, inc=1, device_id=to, device_id_type=pl.DeviceIdType.MESH)

    me = NZ * y + z
    for a, src in enumerate((x_in, g_in)):
        xg[a, at_rows(me, main, main * c), :] = src[0:main, :]
        last = src[main:rows, :].astype(F32)
        none = jnp.zeros_like(last)
        tail[a] = jnp.concatenate(
            [jnp.where(c == 0, last, none), jnp.where(c == 0, none, last)], axis=0
        ).astype(BF16)
    pl.semaphore_wait(barrier, len(greeted))

    for a in range(2):
        mine = xg.at[a, at_rows(me, main, main * c), :]
        send(mine, mine, core_ss.at[a, 0], core_rs.at[a, 0], partner)
        send(tail.at[a], ptail.at[a], core_ss.at[a, 1], core_rs.at[a, 1], partner)

    u, v = frame(c)
    pu, pv = frame(1 - c)
    GROUPS = (0, -1, 1, 2)

    def columns(w, cc, part=None):
        slab, start, count = PARTS[w]
        size = count * quarter if part is None else count * quarter // 2
        col = start * quarter + cc * count * quarter + (0 if part is None else part * size)
        return pl.ds(pl.multiple_of(col, 512), size)

    def region(w, ou, ov, part=None):
        return xg.at[PARTS[w][0], at_rows(slot(c, ring(u, ou), ring(v, ov))), columns(w, c, part)]

    def partner_region(w, ou, ov):
        return xg.at[PARTS[w][0], at_rows(slot(1 - c, ring(pu, ou), ring(pv, ov))), columns(w, 1 - c)]

    def place(label):
        if label < 4:
            base, kind, axis = 0, label, 0
        else:
            base, kind, axis = GROUPS[(label - 4) // 4], label % 4, 1
        off = (-1, 1, 2, 2)[kind]
        part = (None, None, 0, 1)[kind]
        return (off, 0, part) if axis == 0 else (base, off, part)

    def arrived(a, label):
        where = region(a, *place(label))
        rcopy(where, where, ag_ss.at[a, label], ag_rs.at[a, label], partner).wait_recv()

    def pass_on(a, label, where, to):
        send(where, where, ag_ss.at[a, label], ag_rs.at[a, label], to)

    u_plus, u_minus = uv_dev(ring(u, 1), v), uv_dev(ring(u, -1), v)
    v_plus, v_minus = uv_dev(u, ring(v, 1)), uv_dev(u, ring(v, -1))

    def share(a, ou, ov):
        n = 4 * (ou % 4) + ov % 4
        where = region(a, ou, ov)
        send(where, where, sh_ss.at[a, n], sh_rs.at[a, n], partner)

    def along_v(a, r):
        where = region(a, GROUPS[r], 0)
        pass_on(a, 4 + 4 * r, where, v_plus)
        pass_on(a, 5 + 4 * r, where, v_minus)

    def gather_steps(a):
        def begin():
            if a < 2:
                mine = xg.at[a, at_rows(me, main, main * (1 - c)), :]
                rcopy(mine, mine, core_ss.at[a, 0], core_rs.at[a, 0], partner).wait_recv()
                rcopy(tail.at[a], ptail.at[a], core_ss.at[a, 1], core_rs.at[a, 1], partner).wait_recv()
                xg[a, at_rows(me, 2 * rest, 2 * main), :] = tail[a] + ptail[a]
            where = region(a, 0, 0)
            pass_on(a, 0, where, u_plus)
            pass_on(a, 1, where, u_minus)
            along_v(a, 0)

        def u_step(kind):
            off = (-1, 1)[kind]
            arrived(a, kind)
            pass_on(a, 2 + kind, region(a, off, 0, kind), (u_plus, u_minus)[kind])
            along_v(a, 1 + kind)
            share(a, off, 0)

        def u_last():
            arrived(a, 2)
            arrived(a, 3)
            along_v(a, 3)
            share(a, 2, 0)

        def v_step(r, kind):
            off = (-1, 1)[kind]
            arrived(a, 4 + 4 * r + kind)
            pass_on(a, 6 + 4 * r + kind, region(a, GROUPS[r], off, kind), (v_plus, v_minus)[kind])
            share(a, GROUPS[r], off)

        def v_last(r):
            arrived(a, 6 + 4 * r)
            arrived(a, 7 + 4 * r)
            share(a, GROUPS[r], 2)

        def take():
            for ou in range(4):
                for ov in range(4):
                    if ou or ov:
                        n = 4 * ou + ov
                        where = partner_region(a, ou, ov)
                        rcopy(where, where, sh_ss.at[a, n], sh_rs.at[a, n], partner).wait_recv()

        steps = {"begin": begin, "u0": functools.partial(u_step, 0), "u1": functools.partial(u_step, 1)}
        steps.update(ulast=u_last, take=take)
        for r in range(4):
            for kind in range(2):
                steps[f"v{r}{kind}"] = functools.partial(v_step, r, kind)
            steps[f"vl{r}"] = functools.partial(v_last, r)
        return steps

    steps = [gather_steps(w) for w in range(len(PARTS))]

    def go(w, *names):
        for name in names:
            steps[w][name]()

    go(0, "begin", "u0", "u1", "v00", "v01", "ulast", "v10", "v11", "v20", "v21", "vl0", "v30", "v31", "vl1", "vl2")
    go(1, "begin")
    go(0, "vl3", "take")

    for load in loads[:4]:
        load.wait()
    piece = 256

    def put_transposed(which, n, span, value):
        turned = value.T
        if n == 0:
            lt[which, 0:piece, span] = turned
        else:
            keep = full - piece
            lt[which, piece:full, span] = turned[0:keep]
            side = hid - full
            lt[which, full:hid, span] = jnp.where(
                zh == 0, turned[keep:keep + side], turned[keep + side:keep + 2 * side]
            )

    def gate_piece(i, n):
        span = pl.ds(pl.multiple_of(i * piece, piece), piece)
        slab = xg[0, span, :]
        cols = pl.ds(n * piece, piece)
        gate = jnp.dot(slab, wg[:, cols], preferred_element_type=F32)
        up = jnp.dot(slab, wu[:, cols], preferred_element_type=F32)
        sig = jax.nn.sigmoid(gate)
        act = gate * sig
        fb[span, cols] = act.astype(BF16)
        fa[span, cols] = (up * sig * (1.0 + gate * (1.0 - sig))).astype(BF16)
        put_transposed(HIDDEN, n, span, (act * up).astype(BF16))

    pieces = tokens // piece
    gates = [(i, n) for i in range(pieces) for n in range(2)]

    def gate(count):
        for _ in range(count):
            gate_piece(*gates.pop(0))

    gate(2)
    go(1, "u0", "u1", "v00", "v01")
    gate(2)
    go(1, "ulast", "v10", "v11")
    go(2, "begin")
    gate(1)
    go(1, "v20", "v21", "vl0")
    gate(2)
    go(1, "v30", "v31")
    go(2, "u0")
    go(1, "vl1")
    go(2, "u1")
    gate(1)
    go(2, "v00", "v01")
    gate(1)
    go(1, "vl2", "vl3")
    gate(len(gates))
    go(1, "take")

    def factors(j, xx):
        which, side = JOBS[j]
        side = (0, 1, 1 - zh, zh)[side]
        col = pl.multiple_of(side * half + lax.rem(xx, NX) * block, block)
        return jnp.dot(
            lt[which], xg[1 if which == HIDDEN else 0, :, pl.ds(col, block)],
            preferred_element_type=F32,
        )

    top, low = pl.ds(0, hid // 2), pl.ds(hid // 2, hid // 2)
    R, OPP, L = 0, 1, 2
    opposite = {}

    def multiply_one(j, s):
        own[j, s] = factors(j, x + 1 + s).astype(BF16)

    def send_one(j, s):
        if s == OPP:
            opposite[j] = [
                rcopy(own.at[j, OPP, top], fwd.at[j, 0], x_ss.at[j, 0], x_rs.at[j, 0], right),
                rcopy(own.at[j, OPP, low], fwd.at[j, 1], x_ss.at[j, 1], x_rs.at[j, 1], left),
            ]
            for copy in opposite[j]:
                copy.start()
        elif s == R:
            send(own.at[j, R, low], got.at[j, 0, low], x_ss.at[j, 2], x_rs.at[j, 2], right)
        else:
            send(own.at[j, L, top], got.at[j, 1, top], x_ss.at[j, 3], x_rs.at[j, 3], left)

    def multiply(j):
        def one(s, carry):
            multiply_one(j, s)
            return carry

        lax.fori_loop(0, 3, one, 0)
        for s in (OPP, R, L):
            send_one(j, s)

    def add_on(j):
        for n, (s, part, to) in enumerate(((R, top, right), (L, low, left))):
            rcopy(fwd.at[j, n], fwd.at[j, n], x_ss.at[j, n], x_rs.at[j, n], partner).wait_recv()
            own[j, s, part] = (own[j, s, part].astype(F32) + fwd[j, n].astype(F32)).astype(BF16)
            send(own.at[j, s, part], got.at[j, n, part], x_ss.at[j, 4 + n], x_rs.at[j, 4 + n], to)

    out_rows = (
        (pl.ds(0, full), pl.ds(pl.multiple_of(zh * full, 64), full)),
        (pl.ds(full, hid - full), pl.ds(pl.multiple_of(2 * full + zh * (hid - full), 64), hid - full)),
    )
    in_rows = (
        pl.ds(pl.multiple_of((1 - zh) * full, 64), full),
        pl.ds(pl.multiple_of(2 * full + (1 - zh) * (hid - full), 64), hid - full),
    )
    outs = {HIDDEN: out_d, GATE: out_g, UP: out_u}
    local = []

    def prepare(j):
        for copy in opposite[j]:
            copy.wait_send()
        own[j, OPP] = factors(j, x).astype(BF16)

    def finish(j):
        which, side = JOBS[j]
        for n, (a, b) in enumerate(((top, low), (low, top))):
            rcopy(got.at[j, n, b], got.at[j, n, b], x_ss.at[j, 2 + n], x_rs.at[j, 2 + n], partner).wait_recv()
            rcopy(got.at[j, n, a], got.at[j, n, a], x_ss.at[j, 4 + n], x_rs.at[j, 4 + n], partner).wait_recv()
        total = own[j, OPP].astype(F32) + got[j, 0].astype(F32) + got[j, 1].astype(F32)
        own[j, OPP] = (total * scale).astype(BF16)
        for n, (here, there) in enumerate(out_rows):
            src, dst = own.at[j, OPP, here], outs[which].at[there, :]
            def away():
                return rcopy(src, dst, z_ss.at[which, n], z_rs.at[which, n], across)

            def stay():
                return pltpu.make_async_copy(src, dst, loc_sem.at[which, n])

            if side == OTHER:
                away().start()
            elif side == SAME:
                stay().start()
            else:
                pl.when(zh != side)(lambda: away().start())
                pl.when(zh == side)(lambda: stay().start())
            if side in (OTHER, LOW):
                pending.append(away())
            if side in (SAME, HIGH):
                local.append(stay())

    multiply_one(0, OPP)
    send_one(0, OPP)
    go(2, "ulast", "v10", "v11")
    multiply_one(0, R)
    send_one(0, R)
    go(2, "v20", "v21", "vl0")
    multiply_one(0, L)
    send_one(0, L)
    go(2, "v30", "v31", "vl1", "vl2", "vl3", "take")
    add_on(0)
    for s in (OPP, R, L):
        multiply_one(1, s)
        send_one(1, s)

    loads[4].wait()
    loads[5].wait()

    def grad_piece(i, carry):
        span = pl.ds(pl.multiple_of(i * piece, piece), piece)
        slab = xg[1, span, :]
        for n in range(2):
            cols = pl.ds(n * piece, piece)
            back = nt(slab, wd[cols, :])
            gate_grad = (back * fa[span, cols].astype(F32)).astype(BF16)
            up_grad = (back * fb[span, cols].astype(F32)).astype(BF16)
            put_transposed(GATE, n, span, gate_grad)
            put_transposed(UP, n, span, up_grad)
            if n:
                lane = lax.broadcasted_iota(jnp.int32, (piece, piece), 1) - (full - piece)
                side = hid - full
                valid = (lane < 0) | ((lane >= side * zh) & (lane < side * (zh + 1)))
                gate_grad = jnp.where(valid, gate_grad, jnp.zeros_like(gate_grad))
                up_grad = jnp.where(valid, up_grad, jnp.zeros_like(up_grad))
            gu[0, span, cols] = gate_grad
            gu[1, span, cols] = up_grad
        return carry

    lax.fori_loop(0, pieces, grad_piece, 0)

    multiply(2)
    add_on(1)
    prepare(0)

    order = (2, 1, 3, 0)
    strip = 512
    strips = half // strip

    def back_piece(k, cc, add):
        buf = (fa, fb)[k % 2]
        uu, vv = frame(cc)
        spans = [at_rows(slot(cc, ring(uu, order[k]), ring(vv, rv))) for rv in range(4)]

        def one(n, carry):
            at = pl.ds(pl.multiple_of(cc * half + n * strip, strip), strip)
            held = pl.ds(pl.multiple_of(n * plane, 16), plane)
            value = sum(
                nt(jnp.concatenate([gu[w, span, :] for span in spans], axis=0), weight[at, :])
                for w, weight in enumerate((wg, wu))
            )
            if add:
                value += pst[k % 2, held, :].astype(F32)
                wd[0:plane, pl.ds(pl.multiple_of((k % 2) * half + n * strip, strip), strip)] = value.astype(BF16)
            else:
                buf[held, :] = value.astype(BF16)
            return carry

        lax.fori_loop(0, strips, one, 0)

    to_partner = []

    def give_piece(k):
        if k >= 2:
            to_partner[k - 2].wait_send()
        back_piece(k, 1 - c, False)
        copy = rcopy((fa, fb)[k % 2], p_hbm.at[k], p_ss.at[k], p_rs.at[k], partner)
        copy.start()
        to_partner.append(copy)

    def fetch(k):
        rcopy(p_hbm.at[k], p_hbm.at[k], p_ss.at[k], p_rs.at[k], partner).wait_recv()
        copy = pltpu.make_async_copy(p_hbm.at[k], pst.at[k % 2], fetch_sem.at[k % 2])
        copy.start()
        return copy

    def spread(k):
        for rv in (2, 1, 3):
            q = 3 * k + rv - 1
            src = s_hbm.at[k, pl.ds(chip * rv, chip), :]
            send(src, r_hbm.at[q], r_ss.at[q], r_rs.at[q], uv_dev(u, ring(v, rv)))

    written = []

    def sum_piece(k, fetched):
        fetched.wait()
        back_piece(k, c, True)
        copy = pltpu.make_async_copy(
            wd.at[pl.ds(0, plane), pl.ds((k % 2) * half, half)], s_hbm.at[k], fetch_sem.at[2 + k % 2]
        )
        copy.start()
        written.append(copy)

    def send_piece(k):
        written[k].wait()
        spread(k)

    give_piece(0)
    give_piece(1)
    finish(0)
    p0 = fetch(0)
    give_piece(2)
    sum_piece(0, p0)
    p1 = fetch(1)
    multiply(3)
    send_piece(0)
    sum_piece(1, p1)
    add_on(2)
    give_piece(3)
    send_piece(1)
    p2 = fetch(2)
    prepare(1)
    finish(1)
    p3 = fetch(3)
    sum_piece(2, p2)
    prepare(2)
    send_piece(2)
    sum_piece(3, p3)
    add_on(3)
    send_piece(3)
    multiply(4)
    multiply(5)
    to_partner[2].wait_send()
    to_partner[3].wait_send()
    finish(2)
    prepare(3)
    prepare(4)

    def collect(arrivals, kept, k):
        places = [
            wd.at[pl.ds(chip * (n // 2 + 2 * (k % 2)), chip), pl.ds((n % 2) * half, half)] for n in range(4)
        ]
        copies = []
        for n, q in enumerate(arrivals):
            rcopy(r_hbm.at[q], r_hbm.at[q], r_ss.at[q], r_rs.at[q], partner).wait_recv()
            copies.append(pltpu.make_async_copy(r_hbm.at[q], places[n], fetch_sem.at[4 + n]))
        if kept is not None:
            copies.append(pltpu.make_async_copy(kept, places[3], fetch_sem.at[7]))
        for copy in copies:
            copy.start()
        for copy in copies:
            copy.wait()
        span = half // 4
        for n in range(4):
            at = pl.ds(n * span, span)
            terms = [place[:, at].astype(F32) for place in places[:len(copies)]]
            if kept is None:
                terms.append(sums[3, :, at].astype(F32))
            sums[k, :, at] = sum(terms).astype(BF16)

    for k in range(4):
        collect([3 * k, 3 * k + 1, 3 * k + 2], s_hbm.at[k, pl.ds(0, chip), :], k)
        r = order[k]
        if r:
            q = 11 + r
            send(sums.at[k], r_hbm.at[q], r_ss.at[q], r_rs.at[q], uv_dev(ring(u, r), v))
        if k == 1:
            add_on(4)
            finish(3)
    prepare(5)
    add_on(5)
    collect([12, 13, 14], None, 4)

    mine = pl.ds(pl.multiple_of(c * half, half), half)
    theirs = pl.ds(pl.multiple_of((1 - c) * half, half), half)
    keep = sums.at[4, pl.ds(pl.multiple_of(main * c, 16), main), :]
    give = sums.at[4, pl.ds(pl.multiple_of(main * (1 - c), 16), main), :]
    ends = sums.at[4, pl.ds(2 * main, 2 * rest), :]
    send(give, ig_main.at[:, mine], o_ss.at[0], o_rs.at[0], partner)
    send(ends, ig_tail.at[:, mine], o_ss.at[1], o_rs.at[1], partner)
    for n, (src, dst) in enumerate(((keep, ig_main.at[:, mine]), (ends, ig_tail.at[:, mine]))):
        copy = pltpu.make_async_copy(src, dst, fetch_sem.at[n])
        copy.start()
        local.append(copy)

    finish(4)
    finish(5)

    for n, (src, dst) in enumerate(((keep, ig_main), (ends, ig_tail))):
        rcopy(src, dst.at[:, theirs], o_ss.at[n], o_rs.at[n], partner).wait_recv()
    for which in (HIDDEN, GATE, UP):
        for n, (here, _) in enumerate(out_rows):
            rcopy(own.at[0, OPP, here], outs[which].at[in_rows[n], :], z_ss.at[which, n], z_rs.at[which, n], partner).wait_recv()
    for copy in pending:
        copy.wait_send()
    for copy in local:
        copy.wait()


def arrange(
    gate_t, up_t, down, ig_main, ig_tail, grad_gate, grad_up, grad_down, input_grad,
    vg, vu, vd, vt, tg, tu, vi, sem,
):
    main = ig_main.shape[0]
    rest = input_grad.shape[0] - main
    core = lax.rem(lax.axis_index("tensor"), 2)
    moves = [
        pltpu.make_async_copy(src, dst, sem.at[n])
        for n, (src, dst) in enumerate(
            ((gate_t, vg), (up_t, vu), (down, vd), (ig_main, vi.at[pl.ds(0, main), :]), (ig_tail, vt))
        )
    ]
    backs = [
        pltpu.make_async_copy(src, dst, sem.at[5 + n])
        for n, (src, dst) in enumerate(((tg, grad_gate), (tu, grad_up), (vd, grad_down), (vi, input_grad)))
    ]
    for move in moves:
        move.start()
    for n, (src, dst) in enumerate(((vg, tg), (vu, tu))):
        moves[n].wait()
        for k in range(src.shape[0] // 128):
            at = pl.ds(k * 128, 128)
            dst[:, at] = src[at, :].T
        backs[n].start()
    moves[2].wait()
    backs[2].start()
    moves[3].wait()
    moves[4].wait()
    ends = vt[...].astype(F32)
    vi[main:, :] = jnp.where(core == 0, ends[0:rest], ends[rest:]).astype(BF16)
    backs[3].start()
    for back in backs:
        back.wait()


def local(inputs, out_grad, w_gate, w_up, w_down):
    _, rows, width = inputs.shape
    units = w_gate.shape[1]
    hid = units // 2
    pad = hid + 64
    tokens = 2 * rows * NY * NZ
    half = width // 2
    block = width // 8
    chip = 2 * rows
    scale = 1.0 / math.sqrt(rows * lax.axis_size("tensor") * lax.axis_size("dp"))
    dma = pltpu.SemaphoreType.DMA
    any_ = pl.BlockSpec(memory_space=pl.ANY)
    vmem = pl.BlockSpec(memory_space=pltpu.VMEM)
    arr = lambda *shape: jax.ShapeDtypeStruct(shape, BF16)
    outs = pl.pallas_call(
        functools.partial(kernel, scale),
        out_shape=(
            arr(units, block), arr(units, block), arr(units, block),
            arr(rows // 16 * 16, width), arr(16, width),
            arr(4, tokens, half // 4), arr(4, tokens // 4, half), arr(NY * NZ - 1, chip, half),
        ),
        in_specs=[vmem, vmem, any_, any_, any_],
        out_specs=(any_,) * 8,
        scratch_shapes=[
            pltpu.VMEM((2, tokens, width), BF16),
            pltpu.VMEM((width, pad), BF16),
            pltpu.VMEM((width, pad), BF16),
            pltpu.VMEM((pad, width), BF16),
            pltpu.VMEM((tokens, pad), BF16),
            pltpu.VMEM((tokens, pad), BF16),
            pltpu.VMEM((3, hid, tokens), BF16),
            pltpu.VMEM((2, tokens, pad), BF16),
            pltpu.VMEM((6, 3, hid, block), BF16),
            pltpu.VMEM((6, 2, hid // 2, block), BF16),
            pltpu.VMEM((6, 2, hid, block), BF16),
            pltpu.VMEM((5, chip, half), BF16),
            pltpu.VMEM((2, tokens, half // 4), BF16),
            pltpu.VMEM((2, 16, width), BF16),
            pltpu.VMEM((2, 16, width), BF16),
            dma((6,)), dma((2, 2)), dma((2, 2)),
            dma((3, 20)), dma((3, 20)), dma((3, 16)), dma((3, 16)),
            dma((6, 6)), dma((6, 6)),
            dma((4,)), dma((4,)), dma((15,)), dma((15,)),
            dma((3, 2)), dma((3, 2)), dma((2,)), dma((2,)),
            dma((3, 2)), dma((8,)),
        ],
        compiler_params=pltpu.CompilerParams(
            collective_id=0, has_side_effects=True, vmem_limit_bytes=63 * 2**20
        ),
        cost_estimate=pl.CostEstimate(
            flops=16 * tokens * width * hid, bytes_accessed=6 * width * units, transcendentals=tokens * hid
        ),
    )(inputs[0], out_grad[0], w_gate, w_up, w_down)
    grad_gate, grad_up, grad_down, input_grad = pl.pallas_call(
        arrange,
        out_shape=(arr(block, units), arr(block, units), arr(units, block), arr(rows, width)),
        in_specs=[any_] * 5,
        out_specs=(any_,) * 4,
        scratch_shapes=[
            pltpu.VMEM((units, block), BF16), pltpu.VMEM((units, block), BF16), pltpu.VMEM((units, block), BF16),
            pltpu.VMEM((16, width), BF16), pltpu.VMEM((block, units), BF16), pltpu.VMEM((block, units), BF16),
            pltpu.VMEM((rows, width), BF16), dma((9,)),
        ],
    )(*outs[:5])
    return (input_grad[None], grad_gate, grad_up, grad_down)


def solution(mesh):
    placed = (
        P("dp", "tensor", None),
        P("dp", "tensor", None),
        P(None, "tensor"),
        P(None, "tensor"),
        P("tensor", None),
    )
    return jax.shard_map(
        local,
        mesh=mesh,
        in_specs=placed,
        out_specs=(
            P("dp", "tensor", None),
            P("dp", "tensor"),
            P("dp", "tensor"),
            P("tensor", "dp"),
        ),
        check_vma=False,
    )
```

```python
import functools
import math

import jax
import jax.numpy as jnp
from jax import lax
from jax.experimental import pallas as pl
from jax.experimental.pallas import tpu as pltpu
from jax.sharding import PartitionSpec as P

BF16 = jnp.bfloat16
F32 = jnp.float32
NX = NY = NZ = 4
NT = (((1,), (1,)), ((), ()))
HIDDEN, GATE, UP = 0, 1, 2
LOW, HIGH, OTHER, SAME = 0, 1, 2, 3
JOBS = ((HIDDEN, LOW), (HIDDEN, HIGH), (GATE, OTHER), (UP, OTHER), (GATE, SAME), (UP, SAME))
PARTS = ((0, 0, 2), (1, 0, 1), (1, 2, 1))


def nt(left, right):
    return lax.dot_general(left, right, NT, preferred_element_type=F32)


def kernel(
    scale, x_in, g_in, wg_hbm, wu_hbm, wd_hbm,
    out_g, out_u, out_d, ig_main, ig_tail, p_hbm, s_hbm, r_hbm,
    xg, wg, wu, wd, fa, fb, lt, gu, own, fwd, got, sums, pst, tail, ptail,
    w_sem, core_ss, core_rs, ag_ss, ag_rs, sh_ss, sh_rs, x_ss, x_rs,
    p_ss, p_rs, r_ss, r_rs, z_ss, z_rs, o_ss, o_rs, loc_sem, fetch_sem,
):
    rows, width = x_in.shape
    half = width // 2
    quarter = half // 2
    main = rows // 16 * 16
    rest = rows - main
    chip = 2 * rows
    tokens = xg.shape[1]
    plane = NZ * chip
    hid = lt.shape[1]
    pad = wg.shape[1]
    full = pad - 128
    block = width // 8

    t = lax.axis_index("tensor")
    d = lax.axis_index("dp")
    c = lax.rem(t, 2)
    y = lax.rem(t // 2, NY)
    zl = t // (2 * NY)
    x = lax.rem(d, NX)
    zh = d // NX
    z = 2 * zh + zl

    def dev(dx, yy, zz, cc):
        xx = lax.rem(x + dx + NX, NX)
        return {"tensor": (lax.rem(zz, 2) * NY + yy) * 2 + cc, "dp": (zz // 2) * NX + xx}

    def ring(v, off):
        return lax.rem(v + off + 4, 4)

    def frame(cc):
        return y + cc * (z - y), z + cc * (y - z)

    def slot(cc, uu, vv):
        yy, zz = uu + cc * (vv - uu), vv + cc * (uu - vv)
        return NZ * yy + zz

    def uv_dev(uu, vv):
        return dev(0, uu + c * (vv - uu), vv + c * (uu - vv), c)

    def at_rows(index, count=chip, offset=0):
        return pl.ds(pl.multiple_of(chip * index + offset, 16), count)

    partner = dev(0, y, z, 1 - c)
    right, left = dev(1, y, z, c), dev(-1, y, z, c)
    across = dev(0, y, ring(z, 2), c)
    pending = []

    def rcopy(src, dst, ss, rs, to):
        return pltpu.make_async_remote_copy(
            src_ref=src, dst_ref=dst, send_sem=ss, recv_sem=rs,
            device_id=to, device_id_type=pl.DeviceIdType.MESH,
        )

    def send(src, dst, ss, rs, to):
        copy = rcopy(src, dst, ss, rs, to)
        copy.start()
        pending.append(copy)
        return copy

    first = pl.ds(pl.multiple_of(zh * full, 128), full)
    shared = pl.ds(2 * full, pad - full)
    loads = [
        pltpu.make_async_copy(wg_hbm.at[:, first], wg.at[:, pl.ds(0, full)], w_sem.at[0]),
        pltpu.make_async_copy(wg_hbm.at[:, shared], wg.at[:, pl.ds(full, pad - full)], w_sem.at[1]),
        pltpu.make_async_copy(wu_hbm.at[:, first], wu.at[:, pl.ds(0, full)], w_sem.at[2]),
        pltpu.make_async_copy(wu_hbm.at[:, shared], wu.at[:, pl.ds(full, pad - full)], w_sem.at[3]),
        pltpu.make_async_copy(wd_hbm.at[first, :], wd.at[pl.ds(0, full), :], w_sem.at[4]),
        pltpu.make_async_copy(wd_hbm.at[shared, :], wd.at[pl.ds(full, pad - full), :], w_sem.at[5]),
    ]
    for load in loads:
        load.start()

    barrier = pltpu.get_barrier_semaphore()
    greeted = [partner, right, left]
    for ry in range(NY):
        for rz in range(NZ):
            if ry or rz:
                greeted.append(dev(0, ring(y, ry), ring(z, rz), c))
    for to in greeted:
        pl.semaphore_signal(barrier, inc=1, device_id=to, device_id_type=pl.DeviceIdType.MESH)

    me = NZ * y + z
    for a, src in enumerate((x_in, g_in)):
        xg[a, at_rows(me, main, main * c), :] = src[0:main, :]
        last = src[main:rows, :].astype(F32)
        none = jnp.zeros_like(last)
        tail[a] = jnp.concatenate(
            [jnp.where(c == 0, last, none), jnp.where(c == 0, none, last)], axis=0
        ).astype(BF16)
    pl.semaphore_wait(barrier, len(greeted))

    for a in range(2):
        mine = xg.at[a, at_rows(me, main, main * c), :]
        send(mine, mine, core_ss.at[a, 0], core_rs.at[a, 0], partner)
        send(tail.at[a], ptail.at[a], core_ss.at[a, 1], core_rs.at[a, 1], partner)

    u, v = frame(c)
    pu, pv = frame(1 - c)
    GROUPS = (0, -1, 1, 2)

    def columns(w, cc, part=None):
        slab, start, count = PARTS[w]
        size = count * quarter if part is None else count * quarter // 2
        col = start * quarter + cc * count * quarter + (0 if part is None else part * size)
        return pl.ds(pl.multiple_of(col, 512), size)

    def region(w, ou, ov, part=None):
        return xg.at[PARTS[w][0], at_rows(slot(c, ring(u, ou), ring(v, ov))), columns(w, c, part)]

    def partner_region(w, ou, ov):
        return xg.at[PARTS[w][0], at_rows(slot(1 - c, ring(pu, ou), ring(pv, ov))), columns(w, 1 - c)]

    def place(label):
        if label < 4:
            base, kind, axis = 0, label, 0
        else:
            base, kind, axis = GROUPS[(label - 4) // 4], label % 4, 1
        off = (-1, 1, 2, 2)[kind]
        part = (None, None, 0, 1)[kind]
        return (off, 0, part) if axis == 0 else (base, off, part)

    def arrived(a, label):
        where = region(a, *place(label))
        rcopy(where, where, ag_ss.at[a, label], ag_rs.at[a, label], partner).wait_recv()

    def pass_on(a, label, where, to):
        send(where, where, ag_ss.at[a, label], ag_rs.at[a, label], to)

    u_plus, u_minus = uv_dev(ring(u, 1), v), uv_dev(ring(u, -1), v)
    v_plus, v_minus = uv_dev(u, ring(v, 1)), uv_dev(u, ring(v, -1))

    def share(a, ou, ov):
        n = 4 * (ou % 4) + ov % 4
        where = region(a, ou, ov)
        send(where, where, sh_ss.at[a, n], sh_rs.at[a, n], partner)

    def along_v(a, r):
        where = region(a, GROUPS[r], 0)
        pass_on(a, 4 + 4 * r, where, v_plus)
        pass_on(a, 5 + 4 * r, where, v_minus)

    def gather_steps(a):
        def begin():
            if a < 2:
                mine = xg.at[a, at_rows(me, main, main * (1 - c)), :]
                rcopy(mine, mine, core_ss.at[a, 0], core_rs.at[a, 0], partner).wait_recv()
                rcopy(tail.at[a], ptail.at[a], core_ss.at[a, 1], core_rs.at[a, 1], partner).wait_recv()
                xg[a, at_rows(me, 2 * rest, 2 * main), :] = tail[a] + ptail[a]
            where = region(a, 0, 0)
            pass_on(a, 0, where, u_plus)
            pass_on(a, 1, where, u_minus)
            along_v(a, 0)

        def u_step(kind):
            off = (-1, 1)[kind]
            arrived(a, kind)
            pass_on(a, 2 + kind, region(a, off, 0, kind), (u_plus, u_minus)[kind])
            along_v(a, 1 + kind)
            share(a, off, 0)

        def u_last():
            arrived(a, 2)
            arrived(a, 3)
            along_v(a, 3)
            share(a, 2, 0)

        def v_step(r, kind):
            off = (-1, 1)[kind]
            arrived(a, 4 + 4 * r + kind)
            pass_on(a, 6 + 4 * r + kind, region(a, GROUPS[r], off, kind), (v_plus, v_minus)[kind])
            share(a, GROUPS[r], off)

        def v_last(r):
            arrived(a, 6 + 4 * r)
            arrived(a, 7 + 4 * r)
            share(a, GROUPS[r], 2)

        def take():
            for ou in range(4):
                for ov in range(4):
                    if ou or ov:
                        n = 4 * ou + ov
                        where = partner_region(a, ou, ov)
                        rcopy(where, where, sh_ss.at[a, n], sh_rs.at[a, n], partner).wait_recv()

        steps = {"begin": begin, "u0": functools.partial(u_step, 0), "u1": functools.partial(u_step, 1)}
        steps.update(ulast=u_last, take=take)
        for r in range(4):
            for kind in range(2):
                steps[f"v{r}{kind}"] = functools.partial(v_step, r, kind)
            steps[f"vl{r}"] = functools.partial(v_last, r)
        return steps

    steps = [gather_steps(w) for w in range(len(PARTS))]

    def go(w, *names):
        for name in names:
            steps[w][name]()

    go(0, "begin", "u0", "u1", "v00", "v01", "ulast", "v10", "v11", "v20", "v21", "vl0", "v30", "v31", "vl1", "vl2")
    go(1, "begin")
    go(0, "vl3", "take")

    for load in loads[:4]:
        load.wait()
    piece = 256

    def put_transposed(which, n, span, value):
        turned = value.T
        if n == 0:
            lt[which, 0:piece, span] = turned
        else:
            keep = full - piece
            lt[which, piece:full, span] = turned[0:keep]
            side = hid - full
            lt[which, full:hid, span] = jnp.where(
                zh == 0, turned[keep:keep + side], turned[keep + side:keep + 2 * side]
            )

    def gate_piece(i, n):
        span = pl.ds(pl.multiple_of(i * piece, piece), piece)
        slab = xg[0, span, :]
        cols = pl.ds(n * piece, piece)
        gate = jnp.dot(slab, wg[:, cols], preferred_element_type=F32)
        up = jnp.dot(slab, wu[:, cols], preferred_element_type=F32)
        sig = jax.nn.sigmoid(gate)
        act = gate * sig
        fb[span, cols] = act.astype(BF16)
        fa[span, cols] = (up * sig * (1.0 + gate * (1.0 - sig))).astype(BF16)
        put_transposed(HIDDEN, n, span, (act * up).astype(BF16))

    pieces = tokens // piece
    gates = [(i, n) for i in range(pieces) for n in range(2)]

    def gate(count):
        for _ in range(count):
            gate_piece(*gates.pop(0))

    gate(2)
    go(1, "u0", "u1", "v00", "v01")
    gate(2)
    go(1, "ulast", "v10", "v11")
    go(2, "begin")
    gate(1)
    go(1, "v20", "v21", "vl0")
    gate(2)
    go(1, "v30", "v31")
    go(2, "u0")
    go(1, "vl1")
    go(2, "u1")
    gate(1)
    go(2, "v00", "v01")
    gate(1)
    go(1, "vl2", "vl3")
    gate(len(gates))
    go(1, "take")

    def factors(j, xx):
        which, side = JOBS[j]
        side = (0, 1, 1 - zh, zh)[side]
        col = pl.multiple_of(side * half + lax.rem(xx, NX) * block, block)
        return jnp.dot(
            lt[which], xg[1 if which == HIDDEN else 0, :, pl.ds(col, block)],
            preferred_element_type=F32,
        )

    top, low = pl.ds(0, hid // 2), pl.ds(hid // 2, hid // 2)
    R, OPP, L = 0, 1, 2
    opposite = {}

    def multiply_one(j, s):
        own[j, s] = factors(j, x + 1 + s).astype(BF16)

    def send_one(j, s):
        if s == OPP:
            opposite[j] = [
                rcopy(own.at[j, OPP, top], fwd.at[j, 0], x_ss.at[j, 0], x_rs.at[j, 0], right),
                rcopy(own.at[j, OPP, low], fwd.at[j, 1], x_ss.at[j, 1], x_rs.at[j, 1], left),
            ]
            for copy in opposite[j]:
                copy.start()
        elif s == R:
            send(own.at[j, R, low], got.at[j, 0, low], x_ss.at[j, 2], x_rs.at[j, 2], right)
        else:
            send(own.at[j, L, top], got.at[j, 1, top], x_ss.at[j, 3], x_rs.at[j, 3], left)

    def multiply(j):
        def one(s, carry):
            multiply_one(j, s)
            return carry

        lax.fori_loop(0, 3, one, 0)
        for s in (OPP, R, L):
            send_one(j, s)

    def add_on(j):
        for n, (s, part, to) in enumerate(((R, top, right), (L, low, left))):
            rcopy(fwd.at[j, n], fwd.at[j, n], x_ss.at[j, n], x_rs.at[j, n], partner).wait_recv()
            own[j, s, part] = (own[j, s, part].astype(F32) + fwd[j, n].astype(F32)).astype(BF16)
            send(own.at[j, s, part], got.at[j, n, part], x_ss.at[j, 4 + n], x_rs.at[j, 4 + n], to)

    out_rows = (
        (pl.ds(0, full), pl.ds(pl.multiple_of(zh * full, 64), full)),
        (pl.ds(full, hid - full), pl.ds(pl.multiple_of(2 * full + zh * (hid - full), 64), hid - full)),
    )
    in_rows = (
        pl.ds(pl.multiple_of((1 - zh) * full, 64), full),
        pl.ds(pl.multiple_of(2 * full + (1 - zh) * (hid - full), 64), hid - full),
    )
    outs = {HIDDEN: out_d, GATE: out_g, UP: out_u}
    local = []

    def prepare(j):
        for copy in opposite[j]:
            copy.wait_send()
        own[j, OPP] = factors(j, x).astype(BF16)

    def finish(j):
        which, side = JOBS[j]
        for n, (a, b) in enumerate(((top, low), (low, top))):
            rcopy(got.at[j, n, b], got.at[j, n, b], x_ss.at[j, 2 + n], x_rs.at[j, 2 + n], partner).wait_recv()
            rcopy(got.at[j, n, a], got.at[j, n, a], x_ss.at[j, 4 + n], x_rs.at[j, 4 + n], partner).wait_recv()
        total = own[j, OPP].astype(F32) + got[j, 0].astype(F32) + got[j, 1].astype(F32)
        own[j, OPP] = (total * scale).astype(BF16)
        for n, (here, there) in enumerate(out_rows):
            src, dst = own.at[j, OPP, here], outs[which].at[there, :]
            def away():
                return rcopy(src, dst, z_ss.at[which, n], z_rs.at[which, n], across)

            def stay():
                return pltpu.make_async_copy(src, dst, loc_sem.at[which, n])

            if side == OTHER:
                away().start()
            elif side == SAME:
                stay().start()
            else:
                pl.when(zh != side)(lambda: away().start())
                pl.when(zh == side)(lambda: stay().start())
            if side in (OTHER, LOW):
                pending.append(away())
            if side in (SAME, HIGH):
                local.append(stay())

    multiply_one(0, OPP)
    send_one(0, OPP)
    go(2, "ulast", "v10", "v11")
    multiply_one(0, R)
    send_one(0, R)
    go(2, "v20", "v21", "vl0")
    multiply_one(0, L)
    send_one(0, L)
    go(2, "v30", "v31", "vl1", "vl2", "vl3", "take")
    add_on(0)
    for s in (OPP, R, L):
        multiply_one(1, s)
        send_one(1, s)

    loads[4].wait()
    loads[5].wait()

    def grad_piece(i, carry):
        span = pl.ds(pl.multiple_of(i * piece, piece), piece)
        slab = xg[1, span, :]
        for n in range(2):
            cols = pl.ds(n * piece, piece)
            back = nt(slab, wd[cols, :])
            gate_grad = (back * fa[span, cols].astype(F32)).astype(BF16)
            up_grad = (back * fb[span, cols].astype(F32)).astype(BF16)
            put_transposed(GATE, n, span, gate_grad)
            put_transposed(UP, n, span, up_grad)
            if n:
                lane = lax.broadcasted_iota(jnp.int32, (piece, piece), 1) - (full - piece)
                side = hid - full
                valid = (lane < 0) | ((lane >= side * zh) & (lane < side * (zh + 1)))
                gate_grad = jnp.where(valid, gate_grad, jnp.zeros_like(gate_grad))
                up_grad = jnp.where(valid, up_grad, jnp.zeros_like(up_grad))
            gu[0, span, cols] = gate_grad
            gu[1, span, cols] = up_grad
        return carry

    lax.fori_loop(0, pieces, grad_piece, 0)

    order = (2, 1, 3, 0)
    strip = 512
    strips = half // strip

    def back_piece(k, cc, add):
        buf = (fa, fb)[k % 2]
        uu, vv = frame(cc)
        spans = [at_rows(slot(cc, ring(uu, order[k]), ring(vv, rv))) for rv in range(4)]

        def one(n, carry):
            at = pl.ds(pl.multiple_of(cc * half + n * strip, strip), strip)
            held = pl.ds(pl.multiple_of(n * plane, 16), plane)
            value = sum(
                nt(jnp.concatenate([gu[w, span, :] for span in spans], axis=0), weight[at, :])
                for w, weight in enumerate((wg, wu))
            )
            if add:
                value += pst[k % 2, held, :].astype(F32)
                wd[0:plane, pl.ds(pl.multiple_of((k % 2) * half + n * strip, strip), strip)] = value.astype(BF16)
            else:
                buf[held, :] = value.astype(BF16)
            return carry

        lax.fori_loop(0, strips, one, 0)

    to_partner = []

    def give_piece(k):
        if k >= 2:
            to_partner[k - 2].wait_send()
        back_piece(k, 1 - c, False)
        copy = rcopy((fa, fb)[k % 2], p_hbm.at[k], p_ss.at[k], p_rs.at[k], partner)
        copy.start()
        to_partner.append(copy)

    def fetch(k):
        rcopy(p_hbm.at[k], p_hbm.at[k], p_ss.at[k], p_rs.at[k], partner).wait_recv()
        copy = pltpu.make_async_copy(p_hbm.at[k], pst.at[k % 2], fetch_sem.at[k % 2])
        copy.start()
        return copy

    def spread(k):
        for rv in (2, 1, 3):
            q = 3 * k + rv - 1
            src = s_hbm.at[k, pl.ds(chip * rv, chip), :]
            send(src, r_hbm.at[q], r_ss.at[q], r_rs.at[q], uv_dev(u, ring(v, rv)))

    written = []

    def sum_piece(k, fetched):
        fetched.wait()
        back_piece(k, c, True)
        copy = pltpu.make_async_copy(
            wd.at[pl.ds(0, plane), pl.ds((k % 2) * half, half)], s_hbm.at[k], fetch_sem.at[2 + k % 2]
        )
        copy.start()
        written.append(copy)

    def send_piece(k):
        written[k].wait()
        spread(k)

    give_piece(0)
    multiply(2)
    add_on(1)
    prepare(0)
    give_piece(1)
    p0 = fetch(0)
    finish(0)
    sum_piece(0, p0)
    p1 = fetch(1)
    give_piece(2)
    send_piece(0)
    multiply(3)
    sum_piece(1, p1)
    add_on(2)
    give_piece(3)
    send_piece(1)
    p2 = fetch(2)
    prepare(1)
    finish(1)
    p3 = fetch(3)
    sum_piece(2, p2)
    prepare(2)
    send_piece(2)
    sum_piece(3, p3)
    add_on(3)
    send_piece(3)
    multiply(4)
    multiply(5)
    to_partner[2].wait_send()
    to_partner[3].wait_send()
    finish(2)
    prepare(3)
    prepare(4)

    def collect(arrivals, kept, k):
        places = [
            wd.at[pl.ds(chip * (n // 2 + 2 * (k % 2)), chip), pl.ds((n % 2) * half, half)] for n in range(4)
        ]
        copies = []
        for n, q in enumerate(arrivals):
            rcopy(r_hbm.at[q], r_hbm.at[q], r_ss.at[q], r_rs.at[q], partner).wait_recv()
            copies.append(pltpu.make_async_copy(r_hbm.at[q], places[n], fetch_sem.at[4 + n]))
        if kept is not None:
            copies.append(pltpu.make_async_copy(kept, places[3], fetch_sem.at[7]))
        for copy in copies:
            copy.start()
        for copy in copies:
            copy.wait()
        span = half // 4
        for n in range(4):
            at = pl.ds(n * span, span)
            terms = [place[:, at].astype(F32) for place in places[:len(copies)]]
            if kept is None:
                terms.append(sums[3, :, at].astype(F32))
            sums[k, :, at] = sum(terms).astype(BF16)

    for k in range(4):
        collect([3 * k, 3 * k + 1, 3 * k + 2], s_hbm.at[k, pl.ds(0, chip), :], k)
        r = order[k]
        if r:
            q = 11 + r
            send(sums.at[k], r_hbm.at[q], r_ss.at[q], r_rs.at[q], uv_dev(ring(u, r), v))
        if k == 1:
            add_on(4)
            finish(3)
    prepare(5)
    add_on(5)
    collect([12, 13, 14], None, 4)

    mine = pl.ds(pl.multiple_of(c * half, half), half)
    theirs = pl.ds(pl.multiple_of((1 - c) * half, half), half)
    keep = sums.at[4, pl.ds(pl.multiple_of(main * c, 16), main), :]
    give = sums.at[4, pl.ds(pl.multiple_of(main * (1 - c), 16), main), :]
    ends = sums.at[4, pl.ds(2 * main, 2 * rest), :]
    send(give, ig_main.at[:, mine], o_ss.at[0], o_rs.at[0], partner)
    send(ends, ig_tail.at[:, mine], o_ss.at[1], o_rs.at[1], partner)
    for n, (src, dst) in enumerate(((keep, ig_main.at[:, mine]), (ends, ig_tail.at[:, mine]))):
        copy = pltpu.make_async_copy(src, dst, fetch_sem.at[n])
        copy.start()
        local.append(copy)

    finish(4)
    finish(5)

    for n, (src, dst) in enumerate(((keep, ig_main), (ends, ig_tail))):
        rcopy(src, dst.at[:, theirs], o_ss.at[n], o_rs.at[n], partner).wait_recv()
    for which in (HIDDEN, GATE, UP):
        for n, (here, _) in enumerate(out_rows):
            rcopy(own.at[0, OPP, here], outs[which].at[in_rows[n], :], z_ss.at[which, n], z_rs.at[which, n], partner).wait_recv()
    for copy in pending:
        copy.wait_send()
    for copy in local:
        copy.wait()


def arrange(
    gate_t, up_t, down, ig_main, ig_tail, grad_gate, grad_up, grad_down, input_grad,
    vg, vu, vd, vt, tg, tu, vi, sem,
):
    main = ig_main.shape[0]
    rest = input_grad.shape[0] - main
    core = lax.rem(lax.axis_index("tensor"), 2)
    moves = [
        pltpu.make_async_copy(src, dst, sem.at[n])
        for n, (src, dst) in enumerate(
            ((gate_t, vg), (up_t, vu), (down, vd), (ig_main, vi.at[pl.ds(0, main), :]), (ig_tail, vt))
        )
    ]
    backs = [
        pltpu.make_async_copy(src, dst, sem.at[5 + n])
        for n, (src, dst) in enumerate(((tg, grad_gate), (tu, grad_up), (vd, grad_down), (vi, input_grad)))
    ]
    for move in moves:
        move.start()
    for n, (src, dst) in enumerate(((vg, tg), (vu, tu))):
        moves[n].wait()
        for k in range(src.shape[0] // 128):
            at = pl.ds(k * 128, 128)
            dst[:, at] = src[at, :].T
        backs[n].start()
    moves[2].wait()
    backs[2].start()
    moves[3].wait()
    moves[4].wait()
    ends = vt[...].astype(F32)
    vi[main:, :] = jnp.where(core == 0, ends[0:rest], ends[rest:]).astype(BF16)
    backs[3].start()
    for back in backs:
        back.wait()


def local(inputs, out_grad, w_gate, w_up, w_down):
    _, rows, width = inputs.shape
    units = w_gate.shape[1]
    hid = units // 2
    pad = hid + 64
    tokens = 2 * rows * NY * NZ
    half = width // 2
    block = width // 8
    chip = 2 * rows
    scale = 1.0 / math.sqrt(rows * lax.axis_size("tensor") * lax.axis_size("dp"))
    dma = pltpu.SemaphoreType.DMA
    any_ = pl.BlockSpec(memory_space=pl.ANY)
    vmem = pl.BlockSpec(memory_space=pltpu.VMEM)
    arr = lambda *shape: jax.ShapeDtypeStruct(shape, BF16)
    outs = pl.pallas_call(
        functools.partial(kernel, scale),
        out_shape=(
            arr(units, block), arr(units, block), arr(units, block),
            arr(rows // 16 * 16, width), arr(16, width),
            arr(4, tokens, half // 4), arr(4, tokens // 4, half), arr(NY * NZ - 1, chip, half),
        ),
        in_specs=[vmem, vmem, any_, any_, any_],
        out_specs=(any_,) * 8,
        scratch_shapes=[
            pltpu.VMEM((2, tokens, width), BF16),
            pltpu.VMEM((width, pad), BF16),
            pltpu.VMEM((width, pad), BF16),
            pltpu.VMEM((pad, width), BF16),
            pltpu.VMEM((tokens, pad), BF16),
            pltpu.VMEM((tokens, pad), BF16),
            pltpu.VMEM((3, hid, tokens), BF16),
            pltpu.VMEM((2, tokens, pad), BF16),
            pltpu.VMEM((6, 3, hid, block), BF16),
            pltpu.VMEM((6, 2, hid // 2, block), BF16),
            pltpu.VMEM((6, 2, hid, block), BF16),
            pltpu.VMEM((5, chip, half), BF16),
            pltpu.VMEM((2, tokens, half // 4), BF16),
            pltpu.VMEM((2, 16, width), BF16),
            pltpu.VMEM((2, 16, width), BF16),
            dma((6,)), dma((2, 2)), dma((2, 2)),
            dma((3, 20)), dma((3, 20)), dma((3, 16)), dma((3, 16)),
            dma((6, 6)), dma((6, 6)),
            dma((4,)), dma((4,)), dma((15,)), dma((15,)),
            dma((3, 2)), dma((3, 2)), dma((2,)), dma((2,)),
            dma((3, 2)), dma((8,)),
        ],
        compiler_params=pltpu.CompilerParams(
            collective_id=0, has_side_effects=True, vmem_limit_bytes=63 * 2**20
        ),
        cost_estimate=pl.CostEstimate(
            flops=16 * tokens * width * hid, bytes_accessed=6 * width * units, transcendentals=tokens * hid
        ),
    )(inputs[0], out_grad[0], w_gate, w_up, w_down)
    grad_gate, grad_up, grad_down, input_grad = pl.pallas_call(
        arrange,
        out_shape=(arr(block, units), arr(block, units), arr(units, block), arr(rows, width)),
        in_specs=[any_] * 5,
        out_specs=(any_,) * 4,
        scratch_shapes=[
            pltpu.VMEM((units, block), BF16), pltpu.VMEM((units, block), BF16), pltpu.VMEM((units, block), BF16),
            pltpu.VMEM((16, width), BF16), pltpu.VMEM((block, units), BF16), pltpu.VMEM((block, units), BF16),
            pltpu.VMEM((rows, width), BF16), dma((9,)),
        ],
    )(*outs[:5])
    return (input_grad[None], grad_gate, grad_up, grad_down)


def solution(mesh):
    placed = (
        P("dp", "tensor", None),
        P("dp", "tensor", None),
        P(None, "tensor"),
        P(None, "tensor"),
        P("tensor", None),
    )
    return jax.shard_map(
        local,
        mesh=mesh,
        in_specs=placed,
        out_specs=(
            P("dp", "tensor", None),
            P("dp", "tensor"),
            P("dp", "tensor"),
            P("tensor", "dp"),
        ),
        check_vma=False,
    )
```
